512 devices in a mesh: sub: 4 (over y_hi), gy: 4 (over x), gz: 32 (over z, y_lo, core).
Axes of the slice: x: 4, y: 8 (y_hi: 4, y_lo: 2; y = y_hi * 2 + y_lo), z: 8, core: 2. Of those that a mesh axis runs over, the one named last changes fastest.
Arguments:
- source: float32 [4, 4, 512, 4096], P('sub', None, 'gy', 'gz'), may hold values from -6 to 6
- start_field: float32 [4, 4, 512, 4096], P('sub', None, 'gy', 'gz'), may hold values from -6 to 6
- classes: int32 [4, 4, 512, 4096], P('sub', None, 'gy', 'gz'), may hold values from 0 to 7
- class_table: float32 [8], replicated, may hold values from 0.2 to 5
- chain_place: int32 [4], replicated, may hold values from 0 to 3, as said below
- multipliers: float32 [4, 2, 512, 4096], P('sub', None, 'gy', 'gz'), may hold values from -6 to 6
Outputs:
- temperature: float32 [4, 4, 512, 4096], P('sub', None, 'gy', 'gz')
- new_multipliers: float32 [4, 2, 512, 4096], P('sub', None, 'gy', 'gz')
The draws below stay inside these ranges and needn't reach their ends.
Inputs may be any that keep to these rules, and one draw needn't show every extreme that they name: `chain_place`: each place 0 to 3 occurs once.
All inputs are finite; a program needn't handle non-finite values.
Results may differ from the reference program's by a relative error of at most 0.0003.
Values sent between devices are 32-bit elements; how exact they have to be, the bound alone decides.
A program may use at most 64 MiB of HBM per device.

```python
import math
import jax
import jax.numpy as jnp
from jax import lax

CX = 4
SWEEPS = 4
NCLASS = 8
SUBS = 4
NY = 512
NZ = 4096


def draw_chain_place(key, part):
    key = jax.random.fold_in(key, 11)
    scores = jax.random.randint(key, (SUBS,), 0, 1 << 20, dtype=jnp.int32)
    scores = scores * SUBS + jnp.arange(SUBS, dtype=jnp.int32)
    return jnp.argsort(scores, stable=True).astype(jnp.int32)


def set_ends(drawn, rng, least, high):
    longest = drawn.shape.index(max(drawn.shape))
    spots = []
    for shift in (0, 1):
        where = [jax.random.randint(jax.random.fold_in(rng, axis), (), 0, length) for axis, length in enumerate(drawn.shape)]
        where[longest] = (where[longest] + shift) % drawn.shape[longest]
        spots.append(tuple(where))
    return drawn.at[spots[0]].set(least).at[spots[1]].set(high)


def levels(key, extent, cuts, smallest, high):
    def one(dim, parts):
        draws = jax.random.uniform(jax.random.fold_in(jax.random.fold_in(key, 6), dim), (parts,), jnp.float32, smallest / len(cuts), high / len(cuts))
        return jnp.repeat(jnp.exp(draws), extent[dim] // parts).reshape((-1,) + (1,) * (len(extent) - dim - 1))

    gain = one(*cuts[0])
    for cut in cuts[1:]:
        gain = gain * one(*cut)
    return gain


def normal_values(key, extent, deviation, most, split=(), kind=jnp.bfloat16):
    array = jax.random.normal(key, extent, jnp.float32) * deviation
    if len(split) > 0:
        array = levels(key, extent, split, -0.22, 0.18) * array
    return jnp.clip(array, min=-most, max=most).astype(kind)


def setup_inputs(seed: int = 0) -> dict:
    seeds = jax.random.split(jax.random.key(seed), 7)
    source = normal_values(seeds[0], (SUBS, CX, NY, NZ), 1.0, 6.0, ((0, 4), (2, 4), (3, 32)), jnp.float32)
    start_field = normal_values(seeds[1], (SUBS, CX, NY, NZ), 1.0, 6.0, ((0, 4), (2, 4), (3, 32)), jnp.float32)
    classes = set_ends(jax.random.randint(seeds[2], (SUBS, CX, NY, NZ), 0, NCLASS), jax.random.fold_in(seeds[2], 1), 0, NCLASS - 1).astype(jnp.int32)
    class_table = jnp.clip(jnp.exp(jax.random.uniform(seeds[3], (NCLASS,), jnp.float32, math.log(0.2), math.log(5.0))), 0.2, 5.0)
    chain_place = draw_chain_place(jax.random.fold_in(seeds[6], 71), 0)
    multipliers = normal_values(seeds[5], (SUBS, 2, NY, NZ), 1.0, 6.0, ((0, 4), (2, 4), (3, 32)), jnp.float32)
    return dict(source=source, start_field=start_field, classes=classes, class_table=class_table, chain_place=chain_place, multipliers=multipliers)


ROBIN = 1.0
CAPACITY = 0.5
LOW_BOUND = 0.1
HIGH_BOUND = 2.0


def harmonic(first, second):
    return 2.0 * first * second / (first + second)


def conductivity(classes, table):
    total = jnp.zeros(classes.shape, table.dtype)
    for index in range(NCLASS):
        total = total + jnp.where(classes == index, table[index], 0.0)
    return total


def solve_one(source, start_field, classes, mults, has_lower, has_upper, table):
    cond = conductivity(classes, table)
    padded = jnp.pad(cond, ((0, 0), (1, 1), (1, 1)))
    y_next = harmonic(cond, padded[:, 2:, 1:-1])
    y_prev = harmonic(cond, padded[:, :-2, 1:-1])
    z_next = harmonic(cond, padded[:, 1:-1, 2:])
    z_prev = harmonic(cond, padded[:, 1:-1, :-2])
    x_link = harmonic(cond[1:], cond[:-1])
    zero_plane = jnp.zeros_like(cond[:1])
    x_sum = jnp.concatenate([x_link, zero_plane], 0) + jnp.concatenate([zero_plane, x_link], 0)
    layer = lax.broadcasted_iota(jnp.int32, cond.shape, 0)
    lower_coef = jnp.where(has_lower, ROBIN, 2.0 * cond[0])
    upper_coef = jnp.where(has_upper, ROBIN, 2.0 * cond[-1])
    diag = CAPACITY + y_next + y_prev + z_next + z_prev + x_sum
    diag = diag + jnp.where(layer == 0, lower_coef[None], 0.0) + jnp.where(layer == CX - 1, upper_coef[None], 0.0)
    rhs = source + jnp.where(layer == 0, jnp.where(has_lower, mults[0], 0.0)[None], 0.0)
    rhs = rhs + jnp.where(layer == CX - 1, jnp.where(has_upper, mults[1], 0.0)[None], 0.0)

    def apply(field):
        fpad = jnp.pad(field, ((0, 0), (1, 1), (1, 1)))
        near = y_next * fpad[:, 2:, 1:-1] + y_prev * fpad[:, :-2, 1:-1]
        near = near + z_next * fpad[:, 1:-1, 2:] + z_prev * fpad[:, 1:-1, :-2]
        near = near + jnp.concatenate([x_link * field[1:], zero_plane], 0) + jnp.concatenate([zero_plane, x_link * field[:-1]], 0)
        return diag * field - near

    center = (HIGH_BOUND + LOW_BOUND) / 2.0
    half = (HIGH_BOUND - LOW_BOUND) / 2.0
    sigma = center / half
    field = start_field
    resid = rhs - apply(field)
    step = resid / (diag * center)
    rho = 1.0 / sigma
    for sweep in range(SWEEPS):
        field = field + step
        if sweep < SWEEPS - 1:
            resid = resid - apply(step)
            rho_new = 1.0 / (2.0 * sigma - rho)
            step = rho_new * rho * step + (2.0 * rho_new / half) * resid / diag
            rho = rho_new
    packs = jnp.stack([2.0 * ROBIN * field[0] - mults[0], 2.0 * ROBIN * field[-1] - mults[1]])
    return field, packs


def reference(source, start_field, classes, class_table, chain_place, multipliers):
    has_lower = jnp.stack([jnp.any(chain_place == chain_place[s] - 1) for s in range(SUBS)])
    has_upper = jnp.stack([jnp.any(chain_place == chain_place[s] + 1) for s in range(SUBS)])

    def one(items):
        return solve_one(items[0], items[1], items[2], items[3], items[4], items[5], class_table)

    fields, packs = lax.map(one, (source, start_field, classes, multipliers, has_lower, has_upper))
    rows = []
    for s in range(SUBS):
        from_lower = jnp.zeros_like(packs[0, 0])
        from_upper = jnp.zeros_like(packs[0, 0])
        for other in range(SUBS):
            from_lower = from_lower + jnp.where(chain_place[other] == chain_place[s] - 1, packs[other, 1], 0.0)
            from_upper = from_upper + jnp.where(chain_place[other] == chain_place[s] + 1, packs[other, 0], 0.0)
        rows.append(jnp.stack([from_lower, from_upper]))
    return fields, jnp.stack(rows)
```

```python
import jax
import jax.numpy as jnp
from jax import lax
from jax.experimental import pallas as pl
from jax.experimental.pallas import tpu as pltpu
from jax.sharding import PartitionSpec as P

SWEEPS = 4
ROBIN = 1.0
CAPACITY = 0.5
LOW_BOUND = 0.1
HIGH_BOUND = 2.0
MESH = pl.DeviceIdType.MESH

CX = 4
N = 128
TOP = 16
BOTTOM = TOP + N
ROWS = BOTTOM + 16
CHUNKS = ((8, 48), (56, 48), (104, 48))
DIRECTIONS = tuple((dy, dz) for dy in (-1, 0, 1) for dz in (-1, 0, 1) if dy or dz)


def inverse(x):
    guess = pl.reciprocal(x, approx=True)
    return guess * (2.0 - x * guess)


def lookup(classes, splats):
    bit0 = (classes & 1) == 1
    bit1 = (classes & 2) == 2
    bit2 = classes >= 4
    pairs = [jnp.where(bit0, splats[i + 1], splats[i]) for i in range(0, 8, 2)]
    quads = [jnp.where(bit1, pairs[i + 1], pairs[i]) for i in (0, 2)]
    return jnp.where(bit2, quads[1], quads[0])


def kernel(
    source, start, classes, table, chain, mults, t_out, m_out,
    xs, cl, sr, mu, res, hl, hr, pk, hres,
    yn, yp, zn, zp, xn, xp, hyn, hyp, hzn, hzp, hxn, hxp,
    va, vb, hva, hvb, qq, hq, ff, sb, rb,
    load_sem, send_sem, recv_sem, psend, precv,
):
    s = lax.axis_index("sub")
    gy = lax.axis_index("gy")
    gz = lax.axis_index("gz")
    ny = lax.axis_size("gy")
    nz = lax.axis_size("gz")
    subs = lax.axis_size("sub")
    has = {-1: gy > 0, 1: gy < ny - 1}
    hasz = {-1: gz > 0, 1: gz < nz - 1}

    def there(dy, dz):
        ok = None
        for flag in ([has[dy]] if dy else []) + ([hasz[dz]] if dz else []):
            ok = flag if ok is None else jnp.logical_and(ok, flag)
        return ok

    loads = [
        pltpu.make_async_copy(src.at[0], dst.at[:, pl.ds(TOP, N)], load_sem.at[i])
        for i, (src, dst) in enumerate(((start, xs), (classes, cl), (source, sr), (mults, mu)))
    ]
    for copy in loads:
        copy.start()

    barrier = pltpu.get_barrier_semaphore()
    greeted = jnp.int32(subs - 1)
    for dy, dz in DIRECTIONS:
        ok = there(dy, dz)
        greeted = greeted + jnp.where(ok, 1, 0)

        @pl.when(ok)
        def _(dy=dy, dz=dz):
            pl.semaphore_signal(barrier, inc=1, device_id=(s, gy + dy, gz + dz), device_id_type=MESH)

    others = [lax.rem(s + d, subs) for d in range(1, 4)]
    for other in others:
        pl.semaphore_signal(barrier, inc=1, device_id=(other, gy, gz), device_id_type=MESH)

    my_place = chain[s]
    lower = jnp.float32(0.0)
    upper = jnp.float32(0.0)
    for t in range(4):
        lower = lower + jnp.where(chain[t] == my_place - 1, 1.0, 0.0)
        upper = upper + jnp.where(chain[t] == my_place + 1, 1.0, 0.0)

    splats = [jnp.full((8, N), table[i], jnp.float32) for i in range(8)]
    splats = [(0.5 * inverse(v))[:1] for v in splats]

    ones8 = jnp.ones((8, N), jnp.float32)
    for dy, at in ((-1, 8), (1, BOTTOM)):

        @pl.when(jnp.logical_not(has[dy]))
        def _(at=at):
            for l in range(CX):
                xs[l, pl.ds(at, 8)] = ones8
                cl[l, pl.ds(at, 8)] = jnp.ones((8, N), jnp.int32)
                sr[l, pl.ds(at, 8)] = ones8
            for l in range(2):
                mu[l, pl.ds(at, 8)] = ones8
            hl[pl.ds(at, 8)] = ones8
            hr[pl.ds(at, 8)] = ones8

    for dz, ref in ((-1, hl), (1, hr)):

        @pl.when(jnp.logical_not(hasz[dz]))
        def _(ref=ref):
            ref[...] = jnp.ones((ROWS, N), jnp.float32)

    for ref in (va, vb):
        for l in range(CX):
            ref[l, pl.ds(0, 8)] = jnp.zeros((8, N), jnp.float32)
            ref[l, pl.ds(ROWS - 8, 8)] = jnp.zeros((8, N), jnp.float32)
    for ref in (hva, hvb):
        ref[pl.ds(0, 8)] = jnp.zeros((8, N), jnp.float32)
        ref[pl.ds(ROWS - 8, 8)] = jnp.zeros((8, N), jnp.float32)
    for l in range(CX):
        xs[l, pl.ds(0, 8)] = ones8
        xs[l, pl.ds(ROWS - 8, 8)] = ones8
        res[l, pl.ds(0, 8)] = ones8
        res[l, pl.ds(ROWS - 8, 8)] = ones8
    hres[pl.ds(0, 8)] = ones8
    hres[pl.ds(ROWS - 8, 8)] = ones8

    for copy in loads:
        copy.wait()

    lane = lax.broadcasted_iota(jnp.int32, (N, N), 1)
    packed = jnp.zeros((N, N), jnp.float32)
    packed_class = jnp.zeros((N, N), jnp.int32)
    for l in range(CX):
        rhs = sr[l, pl.ds(TOP, N)]
        if l == 0:
            rhs = rhs + lower * mu[0, pl.ds(TOP, N)]
        if l == CX - 1:
            rhs = rhs + upper * mu[1, pl.ds(TOP, N)]
        packed = jnp.where(lane // 8 == l, pltpu.roll(xs[l, pl.ds(TOP, N)], 8 * l + 4, 1), packed)
        packed_class = jnp.where(
            lane // 8 == 4 + l, pltpu.roll(cl[l, pl.ds(TOP, N)], 32 + 8 * l + 4, 1), packed_class
        )
        packed = jnp.where(lane // 8 == 8 + l, pltpu.roll(rhs, 64 + 8 * l + 4, 1), packed)
    pk[...] = jnp.where(lane // 32 == 1, lookup(packed_class, splats), packed)

    pl.semaphore_wait(barrier, greeted)

    sent = []
    k = 0
    for dy, dz in DIRECTIONS:
        own = {-1: 0, 0: 0, 1: N - 8}[dy]
        far = {-1: BOTTOM, 0: TOP, 1: 8}[dy]
        size = N if dy == 0 else 8
        pairs = []
        if dz:
            dst = {-1: hr, 1: hl}[dz]
            pairs.append((pk.at[pl.ds(own, size)], dst.at[pl.ds(far, size)]))
        else:
            for src, dst in ((start, xs), (classes, cl), (source, sr), (mults, mu)):
                pairs.append((src.at[0, :, pl.ds(own, 8)], dst.at[:, pl.ds(far, 8)]))
        for src, dst in pairs:
            copy = pltpu.make_async_remote_copy(
                src_ref=src, dst_ref=dst, send_sem=send_sem.at[k], recv_sem=recv_sem.at[k],
                device_id=(s, gy + dy, gz + dz), device_id_type=MESH,
            )
            pl.when(there(dy, dz))(copy.start)
            sent.append((copy, dy, dz))
            k += 1

    for l in range(CX):
        for r in range(TOP, BOTTOM, 32):
            res[l, pl.ds(r, 32)] = lookup(cl[l, pl.ds(r, 32)], splats)

    for copy, dy, dz in sent:
        pl.when(there(-dy, -dz))(copy.wait_recv)

    for l in range(CX):
        for r in (8, BOTTOM):
            res[l, pl.ds(r, 8)] = lookup(cl[l, pl.ds(r, 8)], splats)

    lane = lax.broadcasted_iota(jnp.int32, (48, N), 1)
    group = lane // 8
    place = lane % 8
    first_lane = lane == 0
    last_lane = lane == N - 1

    def beside(vs, hv):
        edge = None
        nexts, prevs = [], []
        for l in range(CX):
            turned = pltpu.roll(vs[l], 8 * l + 4, 1)
            edge = turned if edge is None else jnp.where(group == l, turned, edge)
            outer = pltpu.roll(hv, N - (8 * l + 4), 1)
            nexts.append(pltpu.roll(jnp.where(first_lane, outer, vs[l]), N - 1, 1))
            prevs.append(pltpu.roll(jnp.where(last_lane, outer, vs[l]), 1, 1))
        hnext = pltpu.roll(jnp.where(place == 4, edge, hv), N - 1, 1)
        hprev = pltpu.roll(jnp.where(place == 3, edge, hv), 1, 1)
        return nexts, prevs, hnext, hprev

    def halo_tile(r, n):
        return jnp.where(place < 4, hl[pl.ds(r, n)], hr[pl.ds(r, n)])

    for r, n in CHUNKS:
        h = halo_tile(r, n)
        hres[pl.ds(r, n)] = jnp.where(lane < 32, pltpu.roll(h, 96, 1), 1.0)
        hva[pl.ds(r, n)] = jnp.where(lane < 32, h, 0.0)

    keep_top = jnp.where(has[-1], 1.0, 0.0)
    keep_bottom = jnp.where(has[1], 1.0, 0.0)
    keep_left = jnp.where(hasz[-1], 1.0, 0.0)
    keep_right = jnp.where(hasz[1], 1.0, 0.0)

    for r, n in CHUNKS:
        row = lax.broadcasted_iota(jnp.int32, (n, N), 0) + r
        rc = [res[l, pl.ds(r, n)] for l in range(CX)]
        hc = hres[pl.ds(r, n)]
        nexts, prevs, hnext, hprev = beside(rc, hc)
        links = [inverse(rc[l] + rc[l + 1]) for l in range(CX - 1)]
        mask_dn = jnp.where(row == BOTTOM - 1, keep_bottom, 1.0)
        mask_up = jnp.where(row == TOP, keep_top, 1.0)
        mask_next = jnp.where(last_lane, keep_right, 1.0)
        mask_prev = jnp.where(first_lane, keep_left, 1.0)
        for l in range(CX):
            a = inverse(rc[l] + res[l, pl.ds(r + 1, n)]) * mask_dn
            b = inverse(rc[l] + res[l, pl.ds(r - 1, n)]) * mask_up
            c = inverse(rc[l] + nexts[l]) * mask_next
            d = inverse(rc[l] + prevs[l]) * mask_prev
            total = CAPACITY + a + b + c + d
            if l > 0:
                total = total + links[l - 1]
            else:
                total = total + (lower * ROBIN + (1.0 - lower) * inverse(rc[l]))
            if l < CX - 1:
                total = total + links[l]
            else:
                total = total + (upper * ROBIN + (1.0 - upper) * inverse(rc[l]))
            e = inverse(total)
            yn[l, pl.ds(r, n)] = a * e
            yp[l, pl.ds(r, n)] = b * e
            zn[l, pl.ds(r, n)] = c * e
            zp[l, pl.ds(r, n)] = d * e
            if l > 0:
                xp[l, pl.ds(r, n)] = links[l - 1] * e
            if l < CX - 1:
                xn[l, pl.ds(r, n)] = links[l] * e
            rhs = sr[l, pl.ds(r, n)]
            if l == 0:
                rhs = rhs + lower * mu[0, pl.ds(r, n)]
            if l == CX - 1:
                rhs = rhs + upper * mu[1, pl.ds(r, n)]
            qq[l, pl.ds(r, n)] = rhs * e
        a = inverse(hc + hres[pl.ds(r + 1, n)]) * mask_dn
        b = inverse(hc + hres[pl.ds(r - 1, n)]) * mask_up
        c = inverse(hc + hnext)
        d = inverse(hc + hprev)
        f = jnp.where(group < CX - 1, inverse(hc + pltpu.roll(hc, N - 8, 1)), 0.0)
        g = jnp.where((group > 0) & (group < CX), inverse(hc + pltpu.roll(hc, 8, 1)), 0.0)
        ends = inverse(hc)
        total = CAPACITY + a + b + c + d + f + g
        total = total + jnp.where(group == 0, lower * ROBIN + (1.0 - lower) * ends, 0.0)
        total = total + jnp.where(group == CX - 1, upper * ROBIN + (1.0 - upper) * ends, 0.0)
        e = inverse(total)
        hyn[pl.ds(r, n)] = a * e
        hyp[pl.ds(r, n)] = b * e
        hzn[pl.ds(r, n)] = c * e
        hzp[pl.ds(r, n)] = d * e
        hxn[pl.ds(r, n)] = f * e
        hxp[pl.ds(r, n)] = g * e
        hq[pl.ds(r, n)] = jnp.where(lane < 32, pltpu.roll(halo_tile(r, n), 64, 1), 0.0) * e

    center = (HIGH_BOUND + LOW_BOUND) / 2.0
    half = (HIGH_BOUND - LOW_BOUND) / 2.0
    sigma = center / half
    rho = 1.0 / sigma
    sends = []
    for sweep in range(SWEEPS):
        if sweep == 0:
            old, hold, new, hnew = xs, hva, va, hvb
            keep, gain = 0.0, 1.0 / center
        else:
            rho_new = 1.0 / (2.0 * sigma - rho)
            keep, gain = rho_new * rho, 2.0 * rho_new / half
            rho = rho_new
            old, hold, new, hnew = ((va, hvb, vb, hva), (vb, hva, va, hvb))[(sweep - 1) % 2]
        last = sweep == SWEEPS - 1
        for part, (r, n) in enumerate(CHUNKS):
            vs = [old[l, pl.ds(r, n)] for l in range(CX)]
            hv = hold[pl.ds(r, n)]
            nexts, prevs, hnext, hprev = beside(vs, hv)
            ends = []
            for l in range(CX):
                near = yn[l, pl.ds(r, n)] * old[l, pl.ds(r + 1, n)]
                near = near + yp[l, pl.ds(r, n)] * old[l, pl.ds(r - 1, n)]
                near = near + zn[l, pl.ds(r, n)] * nexts[l] + zp[l, pl.ds(r, n)] * prevs[l]
                if l > 0:
                    near = near + xp[l, pl.ds(r, n)] * vs[l - 1]
                if l < CX - 1:
                    near = near + xn[l, pl.ds(r, n)] * vs[l + 1]
                q = qq[l, pl.ds(r, n)] - vs[l] + near
                if sweep == 0:
                    step = gain * q
                    field = vs[l] + step
                else:
                    step = keep * vs[l] + gain * q
                    field = ff[l, pl.ds(r, n)] + step
                if last:
                    lo, hi = max(r, TOP), min(r + n, BOTTOM)
                    inner = field[lo - r : hi - r]
                    t_out[0, l, pl.ds(lo - TOP, hi - lo)] = inner
                    if l == 0:
                        ends.append(2.0 * ROBIN * inner - mu[0, pl.ds(lo, hi - lo)])
                    if l == CX - 1:
                        ends.append(2.0 * ROBIN * inner - mu[1, pl.ds(lo, hi - lo)])
                else:
                    qq[l, pl.ds(r, n)] = q
                    new[l, pl.ds(r, n)] = step
                    ff[l, pl.ds(r, n)] = field
            if last:
                for j in (1, 0, 2):
                    above = jnp.where(chain[others[j]] == my_place + 1, 1.0, 0.0)
                    sb[j, pl.ds(lo - TOP, hi - lo)] = above * ends[1] + (1.0 - above) * ends[0]
                    copy = pltpu.make_async_remote_copy(
                        src_ref=sb.at[j, pl.ds(lo - TOP, hi - lo)],
                        dst_ref=rb.at[j, pl.ds(lo - TOP, hi - lo)],
                        send_sem=psend.at[3 * part + j], recv_sem=precv.at[3 * part + j],
                        device_id=(others[j], gy, gz), device_id_type=MESH,
                    )
                    copy.start()
                    sends.append(copy)
            else:
                near = hyn[pl.ds(r, n)] * hold[pl.ds(r + 1, n)] + hyp[pl.ds(r, n)] * hold[pl.ds(r - 1, n)]
                near = near + hzn[pl.ds(r, n)] * hnext + hzp[pl.ds(r, n)] * hprev
                near = near + hxn[pl.ds(r, n)] * pltpu.roll(hv, N - 8, 1) + hxp[pl.ds(r, n)] * pltpu.roll(hv, 8, 1)
                q = hq[pl.ds(r, n)] - hv + near
                hq[pl.ds(r, n)] = q
                hnew[pl.ds(r, n)] = gain * q if sweep == 0 else keep * hv + gain * q

    for copy, dy, dz in sent:
        pl.when(there(dy, dz))(copy.wait_send)
    for copy in sends:
        copy.wait_recv()
    for side, shift in ((0, -1), (1, 1)):
        total = None
        for j in range(3):
            giver = lax.rem(s + subs - (j + 1), subs)
            mine = jnp.where(chain[giver] == my_place + shift, 1.0, 0.0) * rb[j]
            total = mine if total is None else total + mine
        m_out[0, side] = total
    for copy in sends:
        copy.wait_send()


def shards(source, start_field, classes, class_table, chain_place, multipliers):
    wide = pltpu.VMEM((CX, ROWS, N), jnp.float32)
    tall = pltpu.VMEM((ROWS, N), jnp.float32)
    anywhere = pl.BlockSpec(memory_space=pl.ANY)
    scalars = pl.BlockSpec(memory_space=pltpu.SMEM)
    inside = pl.BlockSpec(memory_space=pltpu.VMEM)
    return pl.pallas_call(
        kernel,
        out_shape=(
            jax.ShapeDtypeStruct((1, CX, N, N), jnp.float32),
            jax.ShapeDtypeStruct((1, 2, N, N), jnp.float32),
        ),
        in_specs=[anywhere, anywhere, anywhere, scalars, scalars, anywhere],
        out_specs=(inside, inside),
        scratch_shapes=[
            wide, pltpu.VMEM((CX, ROWS, N), jnp.int32), wide, pltpu.VMEM((2, ROWS, N), jnp.float32),
            wide, tall, tall, pltpu.VMEM((N, N), jnp.float32), tall,
            wide, wide, wide, wide, wide, wide, tall, tall, tall, tall, tall, tall,
            wide, wide, tall, tall, wide, tall, wide,
            pltpu.VMEM((3, N, N), jnp.float32), pltpu.VMEM((3, N, N), jnp.float32),
            pltpu.SemaphoreType.DMA((4,)), pltpu.SemaphoreType.DMA((14,)), pltpu.SemaphoreType.DMA((14,)),
            pltpu.SemaphoreType.DMA((9,)), pltpu.SemaphoreType.DMA((9,)),
        ],
        compiler_params=pltpu.CompilerParams(
            collective_id=0, has_side_effects=True, vmem_limit_bytes=32 * 1024 * 1024
        ),
    )(source, start_field, classes, class_table, chain_place, multipliers)


def solution(mesh):
    blocks = P("sub", None, "gy", "gz")
    return jax.shard_map(
        shards,
        mesh=mesh,
        in_specs=(blocks, blocks, blocks, P(), P(), blocks),
        out_specs=(blocks, blocks),
        check_vma=False,
    )
```

```python
import jax
import jax.numpy as jnp
from jax import lax
from jax.experimental import pallas as pl
from jax.experimental.pallas import tpu as pltpu
from jax.sharding import PartitionSpec as P

SWEEPS = 4
ROBIN = 1.0
CAPACITY = 0.5
LOW_BOUND = 0.1
HIGH_BOUND = 2.0
MESH = pl.DeviceIdType.MESH

CX = 4
N = 128
TOP = 16
BOTTOM = TOP + N
ROWS = BOTTOM + 16
FIRST, COUNT = 8, N + 16
PLANES = 12
DIRECTIONS = ((-1, -1), (-1, 1), (1, -1), (1, 1), (0, 1), (0, -1), (-1, 0), (1, 0))


def inverse(x):
    return pltpu.reciprocal(x, approx=True)


def lookup(classes, splats):
    bit0 = (classes & 1) == 1
    bit1 = (classes & 2) == 2
    bit2 = classes >= 4
    pairs = [jnp.where(bit0, splats[i + 1], splats[i]) for i in range(0, 8, 2)]
    quads = [jnp.where(bit1, pairs[i + 1], pairs[i]) for i in (0, 2)]
    return jnp.where(bit2, quads[1], quads[0])


def lanes(n):
    return lax.broadcasted_iota(jnp.int32, (n, N), 1)


def edge_columns(vs):
    group = lanes(vs[0].shape[0]) // 8
    out = None
    for l in range(CX):
        turned = pltpu.roll(vs[l], 8 * l + 4, 1)
        out = turned if out is None else jnp.where(group == l, turned, out)
    return out


def swapped(edge):
    place = lanes(edge.shape[0]) % 8
    return jnp.where(place == 3, pltpu.roll(edge, N - 1, 1), pltpu.roll(edge, 1, 1))


def kernel(
    source, start, classes, table_hbm, chain_hbm, mults, t_out, m_out,
    table, chain, xs, cl, rh, mu, res, pk, ztx, zrx, crx, ytx, yrx,
    yn, yp, zn, zp, xn, xp, dd, hres, hyn, hyp, hzn, hzp, hxn, hxp,
    v1, v2, v3, h0, h1, h2, h3, qq, hq, sb, rb,
    load_sem, send_sem, recv_sem, psend, precv,
):
    s = lax.axis_index("sub")
    gy = lax.axis_index("gy")
    gz = lax.axis_index("gz")
    ny = lax.axis_size("gy")
    nz = lax.axis_size("gz")
    subs = lax.axis_size("sub")
    has = {-1: gy > 0, 1: gy < ny - 1}
    hasz = {-1: gz > 0, 1: gz < nz - 1}

    def there(dy, dz):
        ok = None
        for flag in ([has[dy]] if dy else []) + ([hasz[dz]] if dz else []):
            ok = flag if ok is None else jnp.logical_and(ok, flag)
        return ok

    loads = [
        pltpu.make_async_copy(src.at[0], dst.at[:, pl.ds(TOP, N)], load_sem.at[i])
        for i, (src, dst) in enumerate(((classes, cl), (start, xs), (source, rh), (mults, mu)))
    ]
    small = [
        pltpu.make_async_copy(table_hbm, table, load_sem.at[4]),
        pltpu.make_async_copy(chain_hbm, chain, load_sem.at[5]),
    ]
    for copy in small + loads:
        copy.start()

    barrier = pltpu.get_barrier_semaphore()
    greeted = jnp.int32(subs - 1)
    for dy, dz in DIRECTIONS:
        ok = there(dy, dz)
        greeted = greeted + jnp.where(ok, 1, 0)

        @pl.when(ok)
        def _(dy=dy, dz=dz):
            pl.semaphore_signal(barrier, inc=1, device_id=(s, gy + dy, gz + dz), device_id_type=MESH)

    others = [lax.rem(s + d, subs) for d in range(1, 4)]
    for other in others:
        pl.semaphore_signal(barrier, inc=1, device_id=(other, gy, gz), device_id_type=MESH)

    ones = jnp.ones((8, N), jnp.float32)
    zeros = jnp.zeros((8, N), jnp.float32)
    endless = jnp.full((8, N), jnp.inf, jnp.float32)
    blank = jnp.where(lanes(8) // 32 == 1, endless, zeros)
    for side, dy in ((0, -1), (1, 1)):

        @pl.when(jnp.logical_not(has[dy]))
        def _(side=side):
            for i in range(PLANES // 2):
                yrx[side, i] = endless if i in (2, 3) else zeros

        for other, dz in ((0, -1), (1, 1)):

            @pl.when(jnp.logical_not(there(dy, dz)))
            def _(k=2 * side + other):
                crx[k] = blank

    for side, dz in ((0, -1), (1, 1)):

        @pl.when(jnp.logical_not(hasz[dz]))
        def _(side=side):
            for r in range(0, N // 2, 8):
                zrx[side, pl.ds(r, 8)] = blank

    for r in (0, 8, BOTTOM, ROWS - 8):
        for l in range(CX):
            for ref in (xs, rh, v1, v2, v3):
                ref[l, pl.ds(r, 8)] = zeros
            res[l, pl.ds(r, 8)] = ones
    for r in (0, ROWS - 8):
        for ref in (h0, h1, h2, h3):
            ref[pl.ds(r, 8)] = zeros
        hres[pl.ds(r, 8)] = ones

    for copy in small:
        copy.wait()
    my_place = chain[s]
    lower = jnp.float32(0.0)
    upper = jnp.float32(0.0)
    for t in range(4):
        lower = lower + jnp.where(chain[t] == my_place - 1, 1.0, 0.0)
        upper = upper + jnp.where(chain[t] == my_place + 1, 1.0, 0.0)

    splats = [0.5 * inverse(jnp.full((8, N), table[i], jnp.float32)) for i in range(8)]
    splats = [v[:1] for v in splats]

    group = lanes(N) // 8
    loads[0].wait()
    for l in range(CX):
        for r in (TOP, BOTTOM - 8):
            res[l, pl.ds(r, 8)] = lookup(cl[l, pl.ds(r, 8)], splats)
    packed = jnp.zeros((N, N), jnp.int32)
    for l in range(CX):
        packed = jnp.where(group == 4 + l, pltpu.roll(cl[l, pl.ds(TOP, N)], 32 + 8 * l + 4, 1), packed)
    packed = jnp.where(group // 4 == 1, lookup(packed, splats), 0.0)
    loads[1].wait()
    for l in range(CX):
        packed = jnp.where(group == l, pltpu.roll(xs[l, pl.ds(TOP, N)], 8 * l + 4, 1), packed)
    loads[2].wait()
    loads[3].wait()
    rh[0, pl.ds(TOP, N)] = rh[0, pl.ds(TOP, N)] + lower * mu[0, pl.ds(TOP, N)]
    rh[CX - 1, pl.ds(TOP, N)] = rh[CX - 1, pl.ds(TOP, N)] + upper * mu[1, pl.ds(TOP, N)]
    for l in range(CX):
        packed = jnp.where(group == 8 + l, pltpu.roll(rh[l, pl.ds(TOP, N)], 64 + 8 * l + 4, 1), packed)
    pk[...] = packed
    half = N // 2
    place = lanes(half) % 8
    ztx[1] = jnp.where(place < 4, packed[:half], pltpu.roll(packed[half:], 4, 1))
    ztx[0] = jnp.where(place < 4, pltpu.roll(packed[half:], N - 4, 1), packed[:half])
    planes = [(ref, l) for ref in (xs, res, rh) for l in range(CX)]
    row = lax.broadcasted_iota(jnp.int32, (8, N), 0)
    for i in range(PLANES // 2):
        (ref, l), (mate, m) = planes[2 * i], planes[2 * i + 1]
        ytx[0, i] = jnp.where(row < 4, ref[l, pl.ds(TOP, 8)], mate[m, pl.ds(TOP - 4, 8)])
        ytx[1, i] = jnp.where(row < 4, ref[l, pl.ds(BOTTOM - 4, 8)], mate[m, pl.ds(BOTTOM - 8, 8)])

    pl.semaphore_wait(barrier, greeted)

    sent = []
    for k, (dy, dz) in enumerate(DIRECTIONS):
        if dy and dz:
            src = pk.at[pl.ds(0 if dy < 0 else N - 8, 8)]
            dst = crx.at[(2 if dy < 0 else 0) + (1 if dz < 0 else 0)]
        elif dz:
            src, dst = ztx.at[0 if dz < 0 else 1], zrx.at[1 if dz < 0 else 0]
        else:
            src, dst = ytx.at[0 if dy < 0 else 1], yrx.at[1 if dy < 0 else 0]
        copy = pltpu.make_async_remote_copy(
            src_ref=src, dst_ref=dst, send_sem=send_sem.at[k], recv_sem=recv_sem.at[k],
            device_id=(s, gy + dy, gz + dz), device_id_type=MESH,
        )
        pl.when(there(dy, dz))(copy.start)
        sent.append((copy, dy, dz))

    for l in range(CX):
        res[l, pl.ds(TOP + 8, N - 16)] = lookup(cl[l, pl.ds(TOP + 8, N - 16)], splats)

    def inner_links(r, n):
        last_lane = lanes(n) == N - 1
        rc = [res[l, pl.ds(r, n)] for l in range(CX)]
        links = [inverse(rc[l] + rc[l + 1]) for l in range(CX - 1)]
        for l in range(CX):
            c = jnp.where(last_lane, 0.0, inverse(rc[l] + pltpu.roll(rc[l], N - 1, 1)))
            d = pltpu.roll(c, 1, 1)
            total = CAPACITY + c + d
            if l > 0:
                total = total + links[l - 1]
            else:
                total = total + (lower * ROBIN + (1.0 - lower) * inverse(rc[l]))
            if l < CX - 1:
                total = total + links[l]
                xn[l, pl.ds(r, n)] = links[l]
            else:
                total = total + (upper * ROBIN + (1.0 - upper) * inverse(rc[l]))
            zn[l, pl.ds(r, n)] = c
            zp[l, pl.ds(r, n)] = d
            dd[l, pl.ds(r, n)] = total
        hyn[pl.ds(r, n)] = swapped(edge_columns(rc))

    inner_links(TOP, N)

    for copy, dy, dz in sent:
        pl.when(there(-dy, -dz))(copy.wait_recv)

    for side, at in ((0, TOP - 4), (1, BOTTOM)):
        for i, (ref, l) in enumerate(planes):
            ref[l, pl.ds(at, 4)] = yrx[side, i // 2, pl.ds(4 * (i % 2), 4)]
    for r in (FIRST, BOTTOM):
        inner_links(r, 8)

    r, n = FIRST, COUNT
    lane = lanes(n)
    group = lane // 8
    place = lane % 8
    first_lane = lane == 0
    last_lane = lane == N - 1

    low, high = zrx[0], zrx[1]
    near_place = lanes(half) % 8 < 4
    small_place = lanes(8) % 8 < 4
    beside_all = jnp.concatenate(
        [
            jnp.where(small_place, crx[0], crx[1]),
            jnp.where(near_place, low, high),
            jnp.where(near_place, pltpu.roll(low, N - 4, 1), pltpu.roll(high, 4, 1)),
            jnp.where(small_place, crx[2], crx[3]),
        ],
        axis=0,
    )
    hc = jnp.where(lane < 32, pltpu.roll(beside_all, 96, 1), 1.0)
    hres[pl.ds(r, n)] = hc
    h0[pl.ds(r, n)] = jnp.where(lane < 32, beside_all, 0.0)
    hrhs = jnp.where(lane < 32, pltpu.roll(beside_all, 64, 1), 0.0)
    gate = jnp.where((place == 3) | (place == 4), inverse(hc + hyn[pl.ds(r, n)]), 0.0)
    c = jnp.where((place == 3) | (place == 7), 0.0, inverse(hc + pltpu.roll(hc, N - 1, 1)))
    d = pltpu.roll(c, 1, 1)
    c = jnp.where(place == 3, gate, c)
    d = jnp.where(place == 4, gate, d)
    a = inverse(hc + hres[pl.ds(r + 1, n)])
    b = inverse(hc + hres[pl.ds(r - 1, n)])
    f = jnp.where(group < CX - 1, inverse(hc + pltpu.roll(hc, N - 8, 1)), 0.0)
    g = jnp.where(group > 0, pltpu.roll(f, 8, 1), 0.0)
    ends = inverse(hc)
    total = CAPACITY + a + b + c + d + f + g
    total = total + jnp.where(group == 0, lower * ROBIN + (1.0 - lower) * ends, 0.0)
    total = total + jnp.where(group == CX - 1, upper * ROBIN + (1.0 - upper) * ends, 0.0)
    e = inverse(total)
    hyn[pl.ds(r, n)] = a * e
    hyp[pl.ds(r, n)] = b * e
    hzn[pl.ds(r, n)] = c * e
    hzp[pl.ds(r, n)] = d * e
    hxn[pl.ds(r, n)] = f * e
    hxp[pl.ds(r, n)] = g * e
    hq[pl.ds(r, n)] = hrhs * e

    gate = swapped(gate)
    links = [xn[l, pl.ds(r, n)] for l in range(CX - 1)]
    for l in range(CX):
        rc = res[l, pl.ds(r, n)]
        across = pltpu.roll(gate, N - (8 * l + 4), 1)
        a = inverse(rc + res[l, pl.ds(r + 1, n)])
        b = inverse(rc + res[l, pl.ds(r - 1, n)])
        e = inverse(dd[l, pl.ds(r, n)] + a + b + jnp.where(first_lane | last_lane, across, 0.0))
        yn[l, pl.ds(r, n)] = a * e
        yp[l, pl.ds(r, n)] = b * e
        zn[l, pl.ds(r, n)] = jnp.where(last_lane, across, zn[l, pl.ds(r, n)]) * e
        zp[l, pl.ds(r, n)] = jnp.where(first_lane, across, zp[l, pl.ds(r, n)]) * e
        if l > 0:
            xp[l, pl.ds(r, n)] = links[l - 1] * e
        if l < CX - 1:
            xn[l, pl.ds(r, n)] = links[l] * e
        qq[l, pl.ds(r, n)] = rh[l, pl.ds(r, n)] * e

    center = (HIGH_BOUND + LOW_BOUND) / 2.0
    half = (HIGH_BOUND - LOW_BOUND) / 2.0
    sigma = center / half
    rho = 1.0 / sigma
    sends = []
    steps = ((xs, h0), (v1, h1), (v2, h2), (v3, h3))
    for sweep in range(SWEEPS):
        if sweep == 0:
            keep, gain = 0.0, 1.0 / center
        else:
            rho_new = 1.0 / (2.0 * sigma - rho)
            keep, gain = rho_new * rho, 2.0 * rho_new / half
            rho = rho_new
        last = sweep == SWEEPS - 1
        old, hold = steps[sweep]
        if last:
            r, n = TOP, N
            lane = lanes(n)
            first_lane = lane == 0
            last_lane = lane == N - 1
        vs = [old[l, pl.ds(r, n)] for l in range(CX)]
        hv = hold[pl.ds(r, n)]
        ends = []
        for l in range(CX):
            outer = pltpu.roll(hv, N - (8 * l + 4), 1)
            near = yn[l, pl.ds(r, n)] * old[l, pl.ds(r + 1, n)]
            near = near + yp[l, pl.ds(r, n)] * old[l, pl.ds(r - 1, n)]
            near = near + zn[l, pl.ds(r, n)] * pltpu.roll(jnp.where(first_lane, outer, vs[l]), N - 1, 1)
            near = near + zp[l, pl.ds(r, n)] * pltpu.roll(jnp.where(last_lane, outer, vs[l]), 1, 1)
            if l > 0:
                near = near + xp[l, pl.ds(r, n)] * vs[l - 1]
            if l < CX - 1:
                near = near + xn[l, pl.ds(r, n)] * vs[l + 1]
            q = qq[l, pl.ds(r, n)] - vs[l] + near
            if last:
                field = xs[l, pl.ds(r, n)] + v1[l, pl.ds(r, n)] + v2[l, pl.ds(r, n)]
                field = field + (vs[l] + (keep * vs[l] + gain * q))
                t_out[0, l] = field
                if l == 0:
                    ends.append(2.0 * ROBIN * field - mu[0, pl.ds(r, n)])
                if l == CX - 1:
                    ends.append(2.0 * ROBIN * field - mu[1, pl.ds(r, n)])
            else:
                qq[l, pl.ds(r, n)] = q
                steps[sweep + 1][0][l, pl.ds(r, n)] = gain * q if sweep == 0 else keep * vs[l] + gain * q
        if not last:
            edge = edge_columns(vs)
            near = hyn[pl.ds(r, n)] * hold[pl.ds(r + 1, n)] + hyp[pl.ds(r, n)] * hold[pl.ds(r - 1, n)]
            near = near + hzn[pl.ds(r, n)] * pltpu.roll(jnp.where(place == 4, edge, hv), N - 1, 1)
            near = near + hzp[pl.ds(r, n)] * pltpu.roll(jnp.where(place == 3, edge, hv), 1, 1)
            near = near + hxn[pl.ds(r, n)] * pltpu.roll(hv, N - 8, 1) + hxp[pl.ds(r, n)] * pltpu.roll(hv, 8, 1)
            q = hq[pl.ds(r, n)] - hv + near
            hq[pl.ds(r, n)] = q
            steps[sweep + 1][1][pl.ds(r, n)] = gain * q if sweep == 0 else keep * hv + gain * q

    for j in (1, 0, 2):
        above = jnp.where(chain[others[j]] == my_place + 1, 1.0, 0.0)
        sb[j] = above * ends[1] + (1.0 - above) * ends[0]
        copy = pltpu.make_async_remote_copy(
            src_ref=sb.at[j], dst_ref=rb.at[j], send_sem=psend.at[j], recv_sem=precv.at[j],
            device_id=(others[j], gy, gz), device_id_type=MESH,
        )
        copy.start()
        sends.append(copy)

    for copy, dy, dz in sent:
        pl.when(there(dy, dz))(copy.wait_send)
    for copy in sends:
        copy.wait_recv()
    for side, shift in ((0, -1), (1, 1)):
        total = None
        for j in range(3):
            giver = lax.rem(s + subs - (j + 1), subs)
            mine = jnp.where(chain[giver] == my_place + shift, 1.0, 0.0) * rb[j]
            total = mine if total is None else total + mine
        m_out[0, side] = total
    for copy in sends:
        copy.wait_send()


def shards(source, start_field, classes, class_table, chain_place, multipliers):
    wide = pltpu.VMEM((CX, ROWS, N), jnp.float32)
    tall = pltpu.VMEM((ROWS, N), jnp.float32)
    outside = pl.BlockSpec(memory_space=pltpu.HBM)
    inside = pl.BlockSpec(memory_space=pltpu.VMEM)
    arrays = (source, start_field, classes, class_table, chain_place, multipliers)
    arrays = [pltpu.with_memory_space_constraint(x, pltpu.HBM) for x in arrays]
    return pl.pallas_call(
        kernel,
        out_shape=(
            pltpu.VMEM((1, CX, N, N), jnp.float32),
            pltpu.VMEM((1, 2, N, N), jnp.float32),
        ),
        in_specs=[outside] * 6,
        out_specs=(inside, inside),
        scratch_shapes=[
            pltpu.SMEM((8,), jnp.float32), pltpu.SMEM((4,), jnp.int32),
            wide, pltpu.VMEM((CX, ROWS, N), jnp.int32), wide, pltpu.VMEM((2, ROWS, N), jnp.float32), wide,
            pltpu.VMEM((N, N), jnp.float32),
            pltpu.VMEM((2, N // 2, N), jnp.float32), pltpu.VMEM((2, N // 2, N), jnp.float32),
            pltpu.VMEM((4, 8, N), jnp.float32),
            pltpu.VMEM((2, PLANES // 2, 8, N), jnp.float32), pltpu.VMEM((2, PLANES // 2, 8, N), jnp.float32),
            wide, wide, wide, wide, wide, wide, wide, tall, tall, tall, tall, tall, tall, tall,
            wide, wide, wide, tall, tall, tall, tall, wide, tall,
            pltpu.VMEM((3, N, N), jnp.float32), pltpu.VMEM((3, N, N), jnp.float32),
            pltpu.SemaphoreType.DMA((6,)), pltpu.SemaphoreType.DMA((8,)), pltpu.SemaphoreType.DMA((8,)),
            pltpu.SemaphoreType.DMA((3,)), pltpu.SemaphoreType.DMA((3,)),
        ],
        compiler_params=pltpu.CompilerParams(
            collective_id=0, has_side_effects=True, vmem_limit_bytes=32 * 1024 * 1024
        ),
    )(*arrays)


def solution(mesh):
    blocks = P("sub", None, "gy", "gz")
    return jax.shard_map(
        shards,
        mesh=mesh,
        in_specs=(blocks, blocks, blocks, P(), P(), blocks),
        out_specs=(blocks, blocks),
        check_vma=False,
    )
```

```python
import jax
import jax.numpy as jnp
from jax import lax
from jax.experimental import pallas as pl
from jax.experimental.pallas import tpu as pltpu
from jax.sharding import PartitionSpec as P

SWEEPS = 4
ROBIN = 1.0
CAPACITY = 0.5
LOW_BOUND = 0.1
HIGH_BOUND = 2.0
MESH = pl.DeviceIdType.MESH

CX = 4
N = 128
TOP = 16
BOTTOM = TOP + N
ROWS = BOTTOM + 16
FIRST, COUNT = 8, N + 16
PLANES = 12
DIRECTIONS = ((-1, -1), (-1, 1), (1, -1), (1, 1), (0, 1), (0, -1), (-1, 0), (1, 0))


def inverse(x):
    return pltpu.reciprocal(x, approx=True)


def lookup(classes, splats):
    bit0 = (classes & 1) == 1
    bit1 = (classes & 2) == 2
    bit2 = classes >= 4
    pairs = [jnp.where(bit0, splats[i + 1], splats[i]) for i in range(0, 8, 2)]
    quads = [jnp.where(bit1, pairs[i + 1], pairs[i]) for i in (0, 2)]
    return jnp.where(bit2, quads[1], quads[0])


def lanes(n):
    return lax.broadcasted_iota(jnp.int32, (n, N), 1)


def edge_columns(vs):
    group = lanes(vs[0].shape[0]) // 8
    out = None
    for l in range(CX):
        turned = pltpu.roll(vs[l], 8 * l + 4, 1)
        out = turned if out is None else jnp.where(group == l, turned, out)
    return out


def swapped(edge):
    place = lanes(edge.shape[0]) % 8
    return jnp.where(place == 3, pltpu.roll(edge, N - 1, 1), pltpu.roll(edge, 1, 1))


def kernel(
    source, start, classes, table_hbm, chain_hbm, mults, t_out, m_out,
    table, chain, xs, cl, rh, mu, res, pk, ztx, zrx, crx, ytx, yrx,
    yn, yp, zn, zp, xn, xp, dd, hres, hyn, hyp, hzn, hzp, hxn, hxp,
    v1, v2, v3, h0, h1, h2, h3, qq, hq, sb, rb,
    load_sem, send_sem, recv_sem, psend, precv,
):
    s = lax.axis_index("sub")
    gy = lax.axis_index("gy")
    gz = lax.axis_index("gz")
    ny = lax.axis_size("gy")
    nz = lax.axis_size("gz")
    subs = lax.axis_size("sub")
    has = {-1: gy > 0, 1: gy < ny - 1}
    hasz = {-1: gz > 0, 1: gz < nz - 1}

    def there(dy, dz):
        ok = None
        for flag in ([has[dy]] if dy else []) + ([hasz[dz]] if dz else []):
            ok = flag if ok is None else jnp.logical_and(ok, flag)
        return ok

    loads = [
        pltpu.make_async_copy(src.at[0], dst.at[:, pl.ds(TOP, N)], load_sem.at[i])
        for i, (src, dst) in enumerate(((classes, cl), (start, xs), (source, rh), (mults, mu)))
    ]
    small = [
        pltpu.make_async_copy(table_hbm, table, load_sem.at[4]),
        pltpu.make_async_copy(chain_hbm, chain, load_sem.at[5]),
    ]
    for copy in small + loads:
        copy.start()

    barrier = pltpu.get_barrier_semaphore()
    greeted = jnp.int32(subs - 1)
    for dy, dz in DIRECTIONS:
        ok = there(dy, dz)
        greeted = greeted + jnp.where(ok, 1, 0)

        @pl.when(ok)
        def _(dy=dy, dz=dz):
            pl.semaphore_signal(barrier, inc=1, device_id=(s, gy + dy, gz + dz), device_id_type=MESH)

    others = [lax.rem(s + d, subs) for d in range(1, 4)]
    for other in others:
        pl.semaphore_signal(barrier, inc=1, device_id=(other, gy, gz), device_id_type=MESH)

    ones = jnp.ones((8, N), jnp.float32)
    zeros = jnp.zeros((8, N), jnp.float32)
    endless = jnp.full((8, N), jnp.inf, jnp.float32)
    blank = jnp.where(lanes(8) // 32 == 1, endless, zeros)
    for side, dy in ((0, -1), (1, 1)):

        @pl.when(jnp.logical_not(has[dy]))
        def _(side=side):
            for i in range(PLANES // 2):
                yrx[side, i] = endless if i in (2, 3) else zeros

        for other, dz in ((0, -1), (1, 1)):

            @pl.when(jnp.logical_not(there(dy, dz)))
            def _(k=2 * side + other):
                crx[k] = blank

    for side, dz in ((0, -1), (1, 1)):

        @pl.when(jnp.logical_not(hasz[dz]))
        def _(side=side):
            for r in range(0, N // 2, 8):
                zrx[side, pl.ds(r, 8)] = blank

    for r in (0, 8, BOTTOM, ROWS - 8):
        for l in range(CX):
            for ref in (xs, rh, v1, v2, v3):
                ref[l, pl.ds(r, 8)] = zeros
            res[l, pl.ds(r, 8)] = ones
    for r in (0, ROWS - 8):
        for ref in (h0, h1, h2, h3):
            ref[pl.ds(r, 8)] = zeros
        hres[pl.ds(r, 8)] = ones

    for copy in small:
        copy.wait()
    my_place = chain[s]
    lower = jnp.float32(0.0)
    upper = jnp.float32(0.0)
    for t in range(4):
        lower = lower + jnp.where(chain[t] == my_place - 1, 1.0, 0.0)
        upper = upper + jnp.where(chain[t] == my_place + 1, 1.0, 0.0)

    splats = [0.5 * inverse(jnp.full((8, N), table[i], jnp.float32)) for i in range(8)]
    splats = [v[:1] for v in splats]

    group = lanes(N) // 8
    loads[0].wait()
    for l in range(CX):
        for r in (TOP, BOTTOM - 8):
            res[l, pl.ds(r, 8)] = lookup(cl[l, pl.ds(r, 8)], splats)
    packed = jnp.zeros((N, N), jnp.int32)
    for l in range(CX):
        packed = jnp.where(group == 4 + l, pltpu.roll(cl[l, pl.ds(TOP, N)], 32 + 8 * l + 4, 1), packed)
    packed = jnp.where(group // 4 == 1, lookup(packed, splats), 0.0)
    loads[1].wait()
    for l in range(CX):
        packed = jnp.where(group == l, pltpu.roll(xs[l, pl.ds(TOP, N)], 8 * l + 4, 1), packed)
    loads[2].wait()
    loads[3].wait()
    rh[0, pl.ds(TOP, N)] = rh[0, pl.ds(TOP, N)] + lower * mu[0, pl.ds(TOP, N)]
    rh[CX - 1, pl.ds(TOP, N)] = rh[CX - 1, pl.ds(TOP, N)] + upper * mu[1, pl.ds(TOP, N)]
    for l in range(CX):
        packed = jnp.where(group == 8 + l, pltpu.roll(rh[l, pl.ds(TOP, N)], 64 + 8 * l + 4, 1), packed)
    pk[...] = packed
    half = N // 2
    place = lanes(half) % 8
    ztx[1] = jnp.where(place < 4, packed[:half], pltpu.roll(packed[half:], 4, 1))
    ztx[0] = jnp.where(place < 4, pltpu.roll(packed[half:], N - 4, 1), packed[:half])
    planes = [(ref, l) for ref in (xs, res, rh) for l in range(CX)]
    row = lax.broadcasted_iota(jnp.int32, (8, N), 0)
    for i in range(PLANES // 2):
        (ref, l), (mate, m) = planes[2 * i], planes[2 * i + 1]
        ytx[0, i] = jnp.where(row < 4, ref[l, pl.ds(TOP, 8)], mate[m, pl.ds(TOP - 4, 8)])
        ytx[1, i] = jnp.where(row < 4, ref[l, pl.ds(BOTTOM - 4, 8)], mate[m, pl.ds(BOTTOM - 8, 8)])

    pl.semaphore_wait(barrier, greeted)

    sent = []
    for k, (dy, dz) in enumerate(DIRECTIONS):
        if dy and dz:
            src = pk.at[pl.ds(0 if dy < 0 else N - 8, 8)]
            dst = crx.at[(2 if dy < 0 else 0) + (1 if dz < 0 else 0)]
        elif dz:
            src, dst = ztx.at[0 if dz < 0 else 1], zrx.at[1 if dz < 0 else 0]
        else:
            src, dst = ytx.at[0 if dy < 0 else 1], yrx.at[1 if dy < 0 else 0]
        copy = pltpu.make_async_remote_copy(
            src_ref=src, dst_ref=dst, send_sem=send_sem.at[k], recv_sem=recv_sem.at[k],
            device_id=(s, gy + dy, gz + dz), device_id_type=MESH,
        )
        pl.when(there(dy, dz))(copy.start)
        sent.append((copy, dy, dz))

    for l in range(CX):
        res[l, pl.ds(TOP + 8, N - 16)] = lookup(cl[l, pl.ds(TOP + 8, N - 16)], splats)

    def inner_links(r, n):
        last_lane = lanes(n) == N - 1
        rc = [res[l, pl.ds(r, n)] for l in range(CX)]
        links = [inverse(rc[l] + rc[l + 1]) for l in range(CX - 1)]
        for l in range(CX):
            c = jnp.where(last_lane, 0.0, inverse(rc[l] + pltpu.roll(rc[l], N - 1, 1)))
            d = pltpu.roll(c, 1, 1)
            total = CAPACITY + c + d
            if l > 0:
                total = total + links[l - 1]
            else:
                total = total + (lower * ROBIN + (1.0 - lower) * inverse(rc[l]))
            if l < CX - 1:
                total = total + links[l]
                xn[l, pl.ds(r, n)] = links[l]
            else:
                total = total + (upper * ROBIN + (1.0 - upper) * inverse(rc[l]))
            zn[l, pl.ds(r, n)] = c
            zp[l, pl.ds(r, n)] = d
            dd[l, pl.ds(r, n)] = total
        hyn[pl.ds(r, n)] = swapped(edge_columns(rc))

    inner_links(TOP, N)

    for copy, dy, dz in sent:
        pl.when(there(-dy, -dz))(copy.wait_recv)

    for side, at in ((0, TOP - 4), (1, BOTTOM)):
        for i, (ref, l) in enumerate(planes):
            ref[l, pl.ds(at, 4)] = yrx[side, i // 2, pl.ds(4 * (i % 2), 4)]
    for r in (FIRST, BOTTOM):
        inner_links(r, 8)

    r, n = FIRST, COUNT
    lane = lanes(n)
    group = lane // 8
    place = lane % 8
    first_lane = lane == 0
    last_lane = lane == N - 1

    low, high = zrx[0], zrx[1]
    near_place = lanes(half) % 8 < 4
    small_place = lanes(8) % 8 < 4
    beside_all = jnp.concatenate(
        [
            jnp.where(small_place, crx[0], crx[1]),
            jnp.where(near_place, low, high),
            jnp.where(near_place, pltpu.roll(low, N - 4, 1), pltpu.roll(high, 4, 1)),
            jnp.where(small_place, crx[2], crx[3]),
        ],
        axis=0,
    )
    hc = jnp.where(lane < 32, pltpu.roll(beside_all, 96, 1), 1.0)
    hres[pl.ds(r, n)] = hc
    h0[pl.ds(r, n)] = jnp.where(lane < 32, beside_all, 0.0)
    hrhs = jnp.where(lane < 32, pltpu.roll(beside_all, 64, 1), 0.0)
    gate = jnp.where((place == 3) | (place == 4), inverse(hc + hyn[pl.ds(r, n)]), 0.0)
    c = jnp.where((place == 3) | (place == 7), 0.0, inverse(hc + pltpu.roll(hc, N - 1, 1)))
    d = pltpu.roll(c, 1, 1)
    c = jnp.where(place == 3, gate, c)
    d = jnp.where(place == 4, gate, d)
    a = inverse(hc + hres[pl.ds(r + 1, n)])
    b = inverse(hc + hres[pl.ds(r - 1, n)])
    f = jnp.where(group < CX - 1, inverse(hc + pltpu.roll(hc, N - 8, 1)), 0.0)
    g = jnp.where(group > 0, pltpu.roll(f, 8, 1), 0.0)
    ends = inverse(hc)
    total = CAPACITY + a + b + c + d + f + g
    total = total + jnp.where(group == 0, lower * ROBIN + (1.0 - lower) * ends, 0.0)
    total = total + jnp.where(group == CX - 1, upper * ROBIN + (1.0 - upper) * ends, 0.0)
    e = inverse(total)
    hyn[pl.ds(r, n)] = a * e
    hyp[pl.ds(r, n)] = b * e
    hzn[pl.ds(r, n)] = c * e
    hzp[pl.ds(r, n)] = d * e
    hxn[pl.ds(r, n)] = f * e
    hxp[pl.ds(r, n)] = g * e
    hq[pl.ds(r, n)] = hrhs * e

    gate = swapped(gate)
    links = [xn[l, pl.ds(r, n)] for l in range(CX - 1)]
    for l in range(CX):
        rc = res[l, pl.ds(r, n)]
        across = pltpu.roll(gate, N - (8 * l + 4), 1)
        a = inverse(rc + res[l, pl.ds(r + 1, n)])
        b = inverse(rc + res[l, pl.ds(r - 1, n)])
        e = inverse(dd[l, pl.ds(r, n)] + a + b + jnp.where(first_lane | last_lane, across, 0.0))
        yn[l, pl.ds(r, n)] = a * e
        yp[l, pl.ds(r, n)] = b * e
        zn[l, pl.ds(r, n)] = jnp.where(last_lane, across, zn[l, pl.ds(r, n)]) * e
        zp[l, pl.ds(r, n)] = jnp.where(first_lane, across, zp[l, pl.ds(r, n)]) * e
        if l > 0:
            xp[l, pl.ds(r, n)] = links[l - 1] * e
        if l < CX - 1:
            xn[l, pl.ds(r, n)] = links[l] * e
        qq[l, pl.ds(r, n)] = rh[l, pl.ds(r, n)] * e

    center = (HIGH_BOUND + LOW_BOUND) / 2.0
    half = (HIGH_BOUND - LOW_BOUND) / 2.0
    sigma = center / half
    rho = 1.0 / sigma
    sends = []
    def send_packs(ends):
        for j in (1, 0, 2):
            above = jnp.where(chain[others[j]] == my_place + 1, 1.0, 0.0)
            sb[j] = above * ends[1] + (1.0 - above) * ends[0]
            copy = pltpu.make_async_remote_copy(
                src_ref=sb.at[j], dst_ref=rb.at[j], send_sem=psend.at[j], recv_sem=precv.at[j],
                device_id=(others[j], gy, gz), device_id_type=MESH,
            )
            copy.start()
            sends.append(copy)

    steps = ((xs, h0), (v1, h1), (v2, h2), (v3, h3))
    for sweep in range(SWEEPS):
        if sweep == 0:
            keep, gain = 0.0, 1.0 / center
        else:
            rho_new = 1.0 / (2.0 * sigma - rho)
            keep, gain = rho_new * rho, 2.0 * rho_new / half
            rho = rho_new
        last = sweep == SWEEPS - 1
        old, hold = steps[sweep]
        if last:
            r, n = TOP, N
            lane = lanes(n)
            first_lane = lane == 0
            last_lane = lane == N - 1
        vs = [old[l, pl.ds(r, n)] for l in range(CX)]
        hv = hold[pl.ds(r, n)]
        ends = []
        for l in (0, CX - 1, 1, 2):
            near = yn[l, pl.ds(r, n)] * old[l, pl.ds(r + 1, n)]
            near = near + yp[l, pl.ds(r, n)] * old[l, pl.ds(r - 1, n)]
            near = near + zn[l, pl.ds(r, n)] * jnp.where(last_lane, pltpu.roll(hv, N - 1 - (8 * l + 4), 1), pltpu.roll(vs[l], N - 1, 1))
            near = near + zp[l, pl.ds(r, n)] * jnp.where(first_lane, pltpu.roll(hv, N - (8 * l + 3), 1), pltpu.roll(vs[l], 1, 1))
            if l > 0:
                near = near + xp[l, pl.ds(r, n)] * vs[l - 1]
            if l < CX - 1:
                near = near + xn[l, pl.ds(r, n)] * vs[l + 1]
            q = qq[l, pl.ds(r, n)] - vs[l] + near
            if last:
                field = xs[l, pl.ds(r, n)] + v1[l, pl.ds(r, n)] + v2[l, pl.ds(r, n)]
                field = field + (vs[l] + (keep * vs[l] + gain * q))
                t_out[0, l] = field
                if l == 0:
                    ends.append(2.0 * ROBIN * field - mu[0, pl.ds(r, n)])
                if l == CX - 1:
                    ends.append(2.0 * ROBIN * field - mu[1, pl.ds(r, n)])
                    send_packs(ends)
            else:
                qq[l, pl.ds(r, n)] = q
                steps[sweep + 1][0][l, pl.ds(r, n)] = gain * q if sweep == 0 else keep * vs[l] + gain * q
        if not last:
            edge = edge_columns(vs)
            near = hyn[pl.ds(r, n)] * hold[pl.ds(r + 1, n)] + hyp[pl.ds(r, n)] * hold[pl.ds(r - 1, n)]
            near = near + hzn[pl.ds(r, n)] * pltpu.roll(jnp.where(place == 4, edge, hv), N - 1, 1)
            near = near + hzp[pl.ds(r, n)] * pltpu.roll(jnp.where(place == 3, edge, hv), 1, 1)
            near = near + hxn[pl.ds(r, n)] * pltpu.roll(hv, N - 8, 1) + hxp[pl.ds(r, n)] * pltpu.roll(hv, 8, 1)
            q = hq[pl.ds(r, n)] - hv + near
            hq[pl.ds(r, n)] = q
            steps[sweep + 1][1][pl.ds(r, n)] = gain * q if sweep == 0 else keep * hv + gain * q

    for copy, dy, dz in sent:
        pl.when(there(dy, dz))(copy.wait_send)
    for copy in sends:
        copy.wait_recv()
    for side, shift in ((0, -1), (1, 1)):
        total = None
        for j in range(3):
            giver = lax.rem(s + subs - (j + 1), subs)
            mine = jnp.where(chain[giver] == my_place + shift, 1.0, 0.0) * rb[j]
            total = mine if total is None else total + mine
        m_out[0, side] = total
    for copy in sends:
        copy.wait_send()


def shards(source, start_field, classes, class_table, chain_place, multipliers):
    wide = pltpu.VMEM((CX, ROWS, N), jnp.float32)
    tall = pltpu.VMEM((ROWS, N), jnp.float32)
    outside = pl.BlockSpec(memory_space=pltpu.HBM)
    inside = pl.BlockSpec(memory_space=pltpu.VMEM)
    arrays = (source, start_field, classes, class_table, chain_place, multipliers)
    arrays = [pltpu.with_memory_space_constraint(x, pltpu.HBM) for x in arrays]
    return pl.pallas_call(
        kernel,
        out_shape=(
            pltpu.VMEM((1, CX, N, N), jnp.float32),
            pltpu.VMEM((1, 2, N, N), jnp.float32),
        ),
        in_specs=[outside] * 6,
        out_specs=(inside, inside),
        scratch_shapes=[
            pltpu.SMEM((8,), jnp.float32), pltpu.SMEM((4,), jnp.int32),
            wide, pltpu.VMEM((CX, ROWS, N), jnp.int32), wide, pltpu.VMEM((2, ROWS, N), jnp.float32), wide,
            pltpu.VMEM((N, N), jnp.float32),
            pltpu.VMEM((2, N // 2, N), jnp.float32), pltpu.VMEM((2, N // 2, N), jnp.float32),
            pltpu.VMEM((4, 8, N), jnp.float32),
            pltpu.VMEM((2, PLANES // 2, 8, N), jnp.float32), pltpu.VMEM((2, PLANES // 2, 8, N), jnp.float32),
            wide, wide, wide, wide, wide, wide, wide, tall, tall, tall, tall, tall, tall, tall,
            wide, wide, wide, tall, tall, tall, tall, wide, tall,
            pltpu.VMEM((3, N, N), jnp.float32), pltpu.VMEM((3, N, N), jnp.float32),
            pltpu.SemaphoreType.DMA((6,)), pltpu.SemaphoreType.DMA((8,)), pltpu.SemaphoreType.DMA((8,)),
            pltpu.SemaphoreType.DMA((3,)), pltpu.SemaphoreType.DMA((3,)),
        ],
        compiler_params=pltpu.CompilerParams(
            collective_id=0, has_side_effects=True, vmem_limit_bytes=32 * 1024 * 1024
        ),
    )(*arrays)


def solution(mesh):
    blocks = P("sub", None, "gy", "gz")
    return jax.shard_map(
        shards,
        mesh=mesh,
        in_specs=(blocks, blocks, blocks, P(), P(), blocks),
        out_specs=(blocks, blocks),
        check_vma=False,
    )
```

```python
import jax
import jax.numpy as jnp
from jax import lax
from jax.experimental import pallas as pl
from jax.experimental.pallas import tpu as pltpu
from jax.sharding import PartitionSpec as P

SWEEPS = 4
ROBIN = 1.0
CAPACITY = 0.5
LOW_BOUND = 0.1
HIGH_BOUND = 2.0
MESH = pl.DeviceIdType.MESH

CX = 4
N = 128
TOP = 16
BOTTOM = TOP + N
ROWS = BOTTOM + 16
FIRST, COUNT = 8, N + 16
QUARTER = N // 4
HIGH = QUARTER + 16
PLANES = 12
DIRECTIONS = ((-1, -1), (-1, 1), (1, -1), (1, 1), (0, 1), (0, -1), (-1, 0), (1, 0))


def inverse(x):
    return pltpu.reciprocal(x, approx=True)


def lookup(classes, splats):
    bit0 = (classes & 1) == 1
    bit1 = (classes & 2) == 2
    bit2 = classes >= 4
    pairs = [jnp.where(bit0, splats[i + 1], splats[i]) for i in range(0, 8, 2)]
    quads = [jnp.where(bit1, pairs[i + 1], pairs[i]) for i in (0, 2)]
    return jnp.where(bit2, quads[1], quads[0])


def lanes(n):
    return lax.broadcasted_iota(jnp.int32, (n, N), 1)


def edge_columns(ref):
    group = lanes(QUARTER) // 8
    body = None
    for k in range(4):
        for l in range(CX):
            turned = pltpu.roll(ref[l, pl.ds(TOP + QUARTER * k, QUARTER)], QUARTER * k + 8 * l + 4, 1)
            body = turned if body is None else jnp.where(group == 4 * k + l, turned, body)
    group = lanes(8) // 8
    above = pltpu.roll(body[QUARTER - 8 :], QUARTER, 1)
    below = pltpu.roll(body[:8], N - QUARTER, 1)
    for l in range(CX):
        above = jnp.where(group == l, pltpu.roll(ref[l, pl.ds(TOP - 8, 8)], 8 * l + 4, 1), above)
        below = jnp.where(group == 12 + l, pltpu.roll(ref[l, pl.ds(BOTTOM, 8)], 96 + 8 * l + 4, 1), below)
    return jnp.concatenate([above, body, below], axis=0)


def turned_in(h, l, whole):
    parts = [pltpu.roll(h[8 : 8 + QUARTER], N - (QUARTER * k + 8 * l + 4), 1) for k in range(4)]
    if whole:
        above = pltpu.roll(h[:8], N - (8 * l + 4), 1)
        below = pltpu.roll(h[8 + QUARTER :], N - (96 + 8 * l + 4), 1)
        parts = [above] + parts + [below]
    return jnp.concatenate(parts, axis=0)


def kernel(
    source, start, classes, table_hbm, chain_hbm, mults, t_out, m_out,
    table, chain, xs, cl, rh, mu, res, ctx, crx, ztx, zrx, ytx, yrx,
    yl, zn, zp, xl, dd, ee, rr, v1, v2, v3, hres, h0, h1, h2, h3, sb, rb,
    load_sem, send_sem, recv_sem, psend, precv,
):
    s = lax.axis_index("sub")
    gy = lax.axis_index("gy")
    gz = lax.axis_index("gz")
    ny = lax.axis_size("gy")
    nz = lax.axis_size("gz")
    subs = lax.axis_size("sub")
    has = {-1: gy > 0, 1: gy < ny - 1}
    hasz = {-1: gz > 0, 1: gz < nz - 1}

    def there(dy, dz):
        ok = None
        for flag in ([has[dy]] if dy else []) + ([hasz[dz]] if dz else []):
            ok = flag if ok is None else jnp.logical_and(ok, flag)
        return ok

    loads = [
        pltpu.make_async_copy(src.at[0], dst.at[:, pl.ds(TOP, N)], load_sem.at[i])
        for i, (src, dst) in enumerate(((classes, cl), (start, xs), (source, rh), (mults, mu)))
    ]
    small = [
        pltpu.make_async_copy(table_hbm, table, load_sem.at[4]),
        pltpu.make_async_copy(chain_hbm, chain, load_sem.at[5]),
    ]
    for copy in small + loads:
        copy.start()

    barrier = pltpu.get_barrier_semaphore()
    greeted = jnp.int32(subs - 1)
    for dy, dz in DIRECTIONS:
        ok = there(dy, dz)
        greeted = greeted + jnp.where(ok, 1, 0)

        @pl.when(ok)
        def _(dy=dy, dz=dz):
            pl.semaphore_signal(barrier, inc=1, device_id=(s, gy + dy, gz + dz), device_id_type=MESH)

    others = [lax.rem(s + d, subs) for d in range(1, 4)]
    for other in others:
        pl.semaphore_signal(barrier, inc=1, device_id=(other, gy, gz), device_id_type=MESH)

    ones = jnp.ones((8, N), jnp.float32)
    zeros = jnp.zeros((8, N), jnp.float32)
    endless = jnp.full((8, N), jnp.inf, jnp.float32)
    blank = jnp.where(lanes(8) // 32 == 1, endless, zeros)
    for side, dy in ((0, -1), (1, 1)):

        @pl.when(jnp.logical_not(has[dy]))
        def _(side=side):
            for i in range(PLANES // 2):
                yrx[side, i] = endless if i in (2, 3) else zeros

        for other, dz in ((0, -1), (1, 1)):

            @pl.when(jnp.logical_not(there(dy, dz)))
            def _(k=2 * side + other):
                crx[k] = blank

    for side, dz in ((0, -1), (1, 1)):

        @pl.when(jnp.logical_not(hasz[dz]))
        def _(side=side):
            for a in range(3):
                for r in range(0, QUARTER // 2, 8):
                    zrx[side, a, pl.ds(r, 8)] = endless if a == 1 else zeros

    for r in (0, 8, BOTTOM, ROWS - 8):
        for l in range(CX):
            for ref in (xs, rh, yl, v1, v2, v3):
                ref[l, pl.ds(r, 8)] = zeros
            res[l, pl.ds(r, 8)] = endless if r in (8, BOTTOM) else ones
    for r in (0, 8 + HIGH):
        for ref in (h0, h1, h2, h3):
            ref[pl.ds(r, 8)] = zeros
        hres[pl.ds(r, 8)] = ones

    for copy in small:
        copy.wait()
    my_place = chain[s]
    lower = jnp.float32(0.0)
    upper = jnp.float32(0.0)
    for t in range(4):
        lower = lower + jnp.where(chain[t] == my_place - 1, 1.0, 0.0)
        upper = upper + jnp.where(chain[t] == my_place + 1, 1.0, 0.0)

    splats = [0.5 * inverse(jnp.full((8, N), table[i], jnp.float32)) for i in range(8)]
    splats = [v[:1] for v in splats]

    lane = lanes(QUARTER)
    group = lane // 8
    place = lane % 8

    def outer_columns(ref):
        packed = None
        for k in range(4):
            for l in range(CX):
                turned = pltpu.roll(ref[l, pl.ds(TOP + QUARTER * k, QUARTER)], QUARTER * k + 8 * l + 4, 1)
                packed = turned if packed is None else jnp.where(group == 4 * k + l, turned, packed)
        return jnp.take_along_axis(packed, lane ^ 7, axis=1)

    loads[0].wait()
    for l in range(CX):
        for r in (TOP, BOTTOM - 8):
            res[l, pl.ds(r, 8)] = lookup(cl[l, pl.ds(r, 8)], splats)
    packed_res = lookup(outer_columns(cl), splats)
    loads[1].wait()
    packed_xs = outer_columns(xs)
    loads[2].wait()
    loads[3].wait()
    rh[0, pl.ds(TOP, N)] = rh[0, pl.ds(TOP, N)] + lower * mu[0, pl.ds(TOP, N)]
    rh[CX - 1, pl.ds(TOP, N)] = rh[CX - 1, pl.ds(TOP, N)] + upper * mu[1, pl.ds(TOP, N)]
    packed_rh = outer_columns(rh)
    half = QUARTER // 2
    near_side = place[:half] < 4
    group8 = lanes(8) // 32
    up_corner = down_corner = None
    for a, packed in enumerate((packed_xs, packed_res, packed_rh)):
        ztx[0, a] = jnp.where(near_side, packed[:half], pltpu.roll(packed[half:], 4, 1))
        ztx[1, a] = jnp.where(near_side, pltpu.roll(packed[half:], N - 4, 1), packed[:half])
        first = packed[:8] if a == 0 else pltpu.roll(packed[:8], 32 * a, 1)
        final = pltpu.roll(packed[QUARTER - 8 :], 32 * a + 32, 1)
        up_corner = first if a == 0 else jnp.where(group8 == a, first, up_corner)
        down_corner = final if a == 0 else jnp.where(group8 == a, final, down_corner)
    ctx[0] = up_corner
    ctx[1] = down_corner
    planes = [(ref, l) for ref in (xs, res, rh) for l in range(CX)]
    row = lax.broadcasted_iota(jnp.int32, (8, N), 0)
    for i in range(PLANES // 2):
        (ref, l), (mate, m) = planes[2 * i], planes[2 * i + 1]
        ytx[0, i] = jnp.where(row < 4, ref[l, pl.ds(TOP, 8)], mate[m, pl.ds(TOP - 4, 8)])
        ytx[1, i] = jnp.where(row < 4, ref[l, pl.ds(BOTTOM - 4, 8)], mate[m, pl.ds(BOTTOM - 8, 8)])

    pl.semaphore_wait(barrier, greeted)

    sent = []
    for k, (dy, dz) in enumerate(DIRECTIONS):
        if dy and dz:
            src = ctx.at[0 if dy < 0 else 1]
            dst = crx.at[(2 if dy < 0 else 0) + (1 if dz < 0 else 0)]
        elif dz:
            src, dst = ztx.at[0 if dz < 0 else 1], zrx.at[1 if dz < 0 else 0]
        else:
            src, dst = ytx.at[0 if dy < 0 else 1], yrx.at[1 if dy < 0 else 0]
        copy = pltpu.make_async_remote_copy(
            src_ref=src, dst_ref=dst, send_sem=send_sem.at[k], recv_sem=recv_sem.at[k],
            device_id=(s, gy + dy, gz + dz), device_id_type=MESH,
        )
        pl.when(there(dy, dz))(copy.start)
        sent.append((copy, dy, dz))

    for l in range(CX):
        res[l, pl.ds(TOP + 8, N - 16)] = lookup(cl[l, pl.ds(TOP + 8, N - 16)], splats)

    def cat(ref, l, blocks, shift=0):
        parts = [ref[l, pl.ds(r + shift, n)] for r, n in blocks]
        return parts[0] if len(parts) == 1 else jnp.concatenate(parts, axis=0)

    def put(ref, l, blocks, value):
        at = 0
        for r, n in blocks:
            ref[l, pl.ds(r, n)] = value[at : at + n]
            at += n

    def inner_part(blocks):
        last_lane = lanes(sum(n for _, n in blocks)) == N - 1
        rc = [cat(res, l, blocks) for l in range(CX)]
        vs = [cat(xs, l, blocks) for l in range(CX)]
        links = [inverse(rc[l] + rc[l + 1]) for l in range(CX - 1)]
        for l in range(CX):
            a = inverse(rc[l] + cat(res, l, blocks, 1))
            b = inverse(rc[l] + cat(res, l, blocks, -1))
            c = jnp.where(last_lane, 0.0, inverse(rc[l] + pltpu.roll(rc[l], N - 1, 1)))
            d = pltpu.roll(c, 1, 1)
            total = CAPACITY + a + b + c + d
            near = a * cat(xs, l, blocks, 1) + b * cat(xs, l, blocks, -1)
            near = near + c * pltpu.roll(vs[l], N - 1, 1) + d * pltpu.roll(vs[l], 1, 1)
            if l > 0:
                total = total + links[l - 1]
                near = near + links[l - 1] * vs[l - 1]
            else:
                total = total + (lower * ROBIN + (1.0 - lower) * inverse(rc[l]))
            if l < CX - 1:
                total = total + links[l]
                near = near + links[l] * vs[l + 1]
                put(xl, l, blocks, links[l])
            else:
                total = total + (upper * ROBIN + (1.0 - upper) * inverse(rc[l]))
            put(yl, l, blocks, a)
            put(zn, l, blocks, c)
            put(zp, l, blocks, d)
            put(dd, l, blocks, total)
            put(rr, l, blocks, cat(rh, l, blocks) - total * vs[l] + near)

    inner_part(((TOP, N),))

    for copy, dy, dz in sent:
        pl.when(there(-dy, -dz))(copy.wait_recv)

    for side, at in ((0, TOP - 4), (1, BOTTOM)):
        for i, (ref, l) in enumerate(planes):
            ref[l, pl.ds(at, 4)] = yrx[side, i // 2, pl.ds(4 * (i % 2), 4)]

    center = (HIGH_BOUND + LOW_BOUND) / 2.0
    half_width = (HIGH_BOUND - LOW_BOUND) / 2.0
    sigma = center / half_width
    rho = 1.0 / sigma

    lane = lanes(HIGH)
    place = lane % 8
    layer = lane // 8 % 4
    near_side = lanes(half) % 8 < 4
    lane8 = lanes(8)
    near8 = lane8 % 8 < 4
    up_corner = jnp.where(near8, crx[1], crx[0])
    down_corner = jnp.where(near8, crx[3], crx[2])
    tiles = []
    for a in range(3):
        low, high = zrx[0, a], zrx[1, a]
        upper_rows = jnp.where(near_side, high, low)
        lower_rows = jnp.where(near_side, pltpu.roll(high, N - 4, 1), pltpu.roll(low, 4, 1))
        above = up_corner if a == 0 else pltpu.roll(up_corner, N - 32 * a, 1)
        above = jnp.where(lane8 < 32, above, pltpu.roll(lower_rows[half - 8 :], 32, 1))
        below = jnp.where(lane8 >= 96, pltpu.roll(down_corner, 96 - 32 * a, 1), pltpu.roll(upper_rows[:8], 96, 1))
        tiles.append(jnp.concatenate([above, upper_rows, lower_rows, below], axis=0))
    hv, hc, hrhs = tiles
    hrows = pl.ds(8, HIGH)
    hres[hrows] = hc
    h0[hrows] = hv
    gate = jnp.where((place == 3) | (place == 4), inverse(hc + edge_columns(res)), 0.0)
    hzn = jnp.where((place == 3) | (place == 7), 0.0, inverse(hc + pltpu.roll(hc, N - 1, 1)))
    hzp = pltpu.roll(hzn, 1, 1)
    hxn = jnp.where(layer < CX - 1, inverse(hc + pltpu.roll(hc, N - 8, 1)), 0.0)
    hxp = pltpu.roll(hxn, 8, 1)
    hyn = inverse(hc + hres[pl.ds(9, HIGH)])
    hyp = inverse(hc + hres[pl.ds(7, HIGH)])
    ends = inverse(hc)
    hd = CAPACITY + hyn + hyp + hzn + hzp + hxn + hxp + gate
    hd = hd + jnp.where(layer == 0, lower * ROBIN + (1.0 - lower) * ends, 0.0)
    hd = hd + jnp.where(layer == CX - 1, upper * ROBIN + (1.0 - upper) * ends, 0.0)
    he = inverse(hd)

    def outer_near(hold, hv, old):
        near = hyn * hold[pl.ds(9, HIGH)] + hyp * hold[pl.ds(7, HIGH)]
        near = near + hzn * pltpu.roll(hv, N - 1, 1) + hzp * pltpu.roll(hv, 1, 1)
        near = near + hxn * pltpu.roll(hv, N - 8, 1) + hxp * pltpu.roll(hv, 8, 1)
        return near + gate * edge_columns(old)

    hr = hrhs - hd * hv + outer_near(h0, hv, xs)
    h1[hrows] = 1.0 / center * (he * hr)

    inner_part(((FIRST, 16), (BOTTOM - 8, 16)))
    r, n = FIRST, COUNT
    lane = lanes(n)
    edge = (lane == 0) | (lane == N - 1)
    flow = gate * hv
    for l in range(CX):
        across = jnp.where(edge, turned_in(gate, l, True), 0.0)
        total = dd[l, pl.ds(r, n)] + across
        e = inverse(total)
        q = rr[l, pl.ds(r, n)] - across * xs[l, pl.ds(r, n)] + jnp.where(edge, turned_in(flow, l, True), 0.0)
        dd[l, pl.ds(r, n)] = total
        ee[l, pl.ds(r, n)] = e
        rr[l, pl.ds(r, n)] = q
        v1[l, pl.ds(r, n)] = 1.0 / center * (e * q)

    sends = []

    def send_packs(ends):
        for j in (1, 0, 2):
            above = jnp.where(chain[others[j]] == my_place + 1, 1.0, 0.0)
            sb[j] = above * ends[1] + (1.0 - above) * ends[0]
            copy = pltpu.make_async_remote_copy(
                src_ref=sb.at[j], dst_ref=rb.at[j], send_sem=psend.at[j], recv_sem=precv.at[j],
                device_id=(others[j], gy, gz), device_id_type=MESH,
            )
            copy.start()
            sends.append(copy)

    steps = ((xs, h0), (v1, h1), (v2, h2), (v3, h3))
    for sweep in range(1, SWEEPS):
        rho_new = 1.0 / (2.0 * sigma - rho)
        keep, gain = rho_new * rho, 2.0 * rho_new / half_width
        rho = rho_new
        last = sweep == SWEEPS - 1
        old, hold = steps[sweep]
        if last:
            r, n = TOP, N
            lane = lanes(n)
            edge = (lane == 0) | (lane == N - 1)
        vs = [old[l, pl.ds(r, n)] for l in range(CX)]
        hv = hold[hrows]
        flow = gate * hv
        ends = []
        for l in (0, CX - 1, 1, 2):
            near = yl[l, pl.ds(r, n)] * old[l, pl.ds(r + 1, n)] + yl[l, pl.ds(r - 1, n)] * old[l, pl.ds(r - 1, n)]
            near = near + zn[l, pl.ds(r, n)] * pltpu.roll(vs[l], N - 1, 1)
            near = near + zp[l, pl.ds(r, n)] * pltpu.roll(vs[l], 1, 1)
            if l > 0:
                near = near + xl[l - 1, pl.ds(r, n)] * vs[l - 1]
            if l < CX - 1:
                near = near + xl[l, pl.ds(r, n)] * vs[l + 1]
            near = near + jnp.where(edge, turned_in(flow, l, not last), 0.0)
            q = rr[l, pl.ds(r, n)] - dd[l, pl.ds(r, n)] * vs[l] + near
            step = keep * vs[l] + gain * (ee[l, pl.ds(r, n)] * q)
            if last:
                field = xs[l, pl.ds(r, n)] + v1[l, pl.ds(r, n)] + v2[l, pl.ds(r, n)]
                field = field + (vs[l] + step)
                t_out[0, l] = field
                if l == 0:
                    ends.append(2.0 * ROBIN * field - mu[0, pl.ds(r, n)])
                if l == CX - 1:
                    ends.append(2.0 * ROBIN * field - mu[1, pl.ds(r, n)])
                    send_packs(ends)
            else:
                rr[l, pl.ds(r, n)] = q
                steps[sweep + 1][0][l, pl.ds(r, n)] = step
        if not last:
            hr = hr - hd * hv + outer_near(hold, hv, old)
            steps[sweep + 1][1][hrows] = keep * hv + gain * (he * hr)

    for copy, dy, dz in sent:
        pl.when(there(dy, dz))(copy.wait_send)
    for copy in sends:
        copy.wait_recv()
    for side, shift in ((0, -1), (1, 1)):
        total = None
        for j in range(3):
            giver = lax.rem(s + subs - (j + 1), subs)
            mine = jnp.where(chain[giver] == my_place + shift, 1.0, 0.0) * rb[j]
            total = mine if total is None else total + mine
        m_out[0, side] = total
    for copy in sends:
        copy.wait_send()


def shards(source, start_field, classes, class_table, chain_place, multipliers):
    wide = pltpu.VMEM((CX, ROWS, N), jnp.float32)
    tall = pltpu.VMEM((HIGH + 16, N), jnp.float32)
    outside = pl.BlockSpec(memory_space=pltpu.HBM)
    inside = pl.BlockSpec(memory_space=pltpu.VMEM)
    arrays = (source, start_field, classes, class_table, chain_place, multipliers)
    arrays = [pltpu.with_memory_space_constraint(x, pltpu.HBM) for x in arrays]
    return pl.pallas_call(
        kernel,
        out_shape=(
            pltpu.VMEM((1, CX, N, N), jnp.float32),
            pltpu.VMEM((1, 2, N, N), jnp.float32),
        ),
        in_specs=[outside] * 6,
        out_specs=(inside, inside),
        scratch_shapes=[
            pltpu.SMEM((8,), jnp.float32), pltpu.SMEM((4,), jnp.int32),
            wide, pltpu.VMEM((CX, ROWS, N), jnp.int32), wide, pltpu.VMEM((2, ROWS, N), jnp.float32), wide,
            pltpu.VMEM((2, 8, N), jnp.float32), pltpu.VMEM((4, 8, N), jnp.float32),
            pltpu.VMEM((2, 3, QUARTER // 2, N), jnp.float32), pltpu.VMEM((2, 3, QUARTER // 2, N), jnp.float32),
            pltpu.VMEM((2, PLANES // 2, 8, N), jnp.float32), pltpu.VMEM((2, PLANES // 2, 8, N), jnp.float32),
            wide, wide, wide, wide, wide, wide, wide, wide, wide, wide, tall, tall, tall, tall, tall,
            pltpu.VMEM((3, N, N), jnp.float32), pltpu.VMEM((3, N, N), jnp.float32),
            pltpu.SemaphoreType.DMA((6,)), pltpu.SemaphoreType.DMA((8,)), pltpu.SemaphoreType.DMA((8,)),
            pltpu.SemaphoreType.DMA((3,)), pltpu.SemaphoreType.DMA((3,)),
        ],
        compiler_params=pltpu.CompilerParams(
            collective_id=0, has_side_effects=True, vmem_limit_bytes=32 * 1024 * 1024
        ),
    )(*arrays)


def solution(mesh):
    blocks = P("sub", None, "gy", "gz")
    return jax.shard_map(
        shards,
        mesh=mesh,
        in_specs=(blocks, blocks, blocks, P(), P(), blocks),
        out_specs=(blocks, blocks),
        check_vma=False,
    )
```

```python
import functools

import jax
import jax.numpy as jnp
from jax import lax
from jax.experimental import pallas as pl
from jax.experimental.pallas import tpu as pltpu
from jax.sharding import PartitionSpec as P

SWEEPS = 4
ROBIN = 1.0
CAPACITY = 0.5
LOW_BOUND = 0.1
HIGH_BOUND = 2.0
MESH = pl.DeviceIdType.MESH

CX = 4
N = 128
TOP = 16
BOTTOM = TOP + N
ROWS = BOTTOM + 16
FIRST, COUNT = 8, N + 16
QUARTER = N // 4
HIGH = QUARTER + 16
PLANES = 12
DIRECTIONS = ((-1, -1), (-1, 1), (1, -1), (1, 1), (0, 1), (0, -1), (-1, 0), (1, 0))


def inverse(x):
    return pltpu.reciprocal(x, approx=True)


def lookup(classes, splats):
    bit0 = (classes & 1) == 1
    bit1 = (classes & 2) == 2
    bit2 = classes >= 4
    pairs = [jnp.where(bit0, splats[i + 1], splats[i]) for i in range(0, 8, 2)]
    quads = [jnp.where(bit1, pairs[i + 1], pairs[i]) for i in (0, 2)]
    return jnp.where(bit2, quads[1], quads[0])


def lanes(n):
    return lax.broadcasted_iota(jnp.int32, (n, N), 1)


def edge_columns(ref):
    group = lanes(QUARTER) // 8
    body = None
    for k in range(4):
        for l in range(CX):
            turned = pltpu.roll(ref[l, pl.ds(TOP + QUARTER * k, QUARTER)], QUARTER * k + 8 * l + 4, 1)
            body = turned if body is None else jnp.where(group == 4 * k + l, turned, body)
    group = lanes(8) // 8
    above = pltpu.roll(body[QUARTER - 8 :], QUARTER, 1)
    below = pltpu.roll(body[:8], N - QUARTER, 1)
    for l in range(CX):
        above = jnp.where(group == l, pltpu.roll(ref[l, pl.ds(TOP - 8, 8)], 8 * l + 4, 1), above)
        below = jnp.where(group == 12 + l, pltpu.roll(ref[l, pl.ds(BOTTOM, 8)], 96 + 8 * l + 4, 1), below)
    return jnp.concatenate([above, body, below], axis=0)


def turned_in(h, l, whole):
    parts = [pltpu.roll(h[8 : 8 + QUARTER], N - (QUARTER * k + 8 * l + 4), 1) for k in range(4)]
    if whole:
        above = pltpu.roll(h[:8], N - (8 * l + 4), 1)
        below = pltpu.roll(h[8 + QUARTER :], N - (96 + 8 * l + 4), 1)
        parts = [above] + parts + [below]
    return jnp.concatenate(parts, axis=0)


def kernel(
    unused, source, start, classes, table_hbm, chain_hbm, mults, t_out, m_out,
    table, chain, xs, cl, rh, mu, res, ctx, crx, ztx, zrx, ytx, yrx,
    yl, zn, zp, xl, dd, ee, rr, v1, v2, v3, hres, h0, h1, h2, h3, sb, rb,
    load_sem, send_sem, recv_sem, psend, precv,
):
    s = lax.axis_index("sub")
    gy = lax.axis_index("gy")
    gz = lax.axis_index("gz")
    ny = lax.axis_size("gy")
    nz = lax.axis_size("gz")
    has = {-1: gy > 0, 1: gy < ny - 1}
    hasz = {-1: gz > 0, 1: gz < nz - 1}

    def there(dy, dz):
        ok = None
        for flag in ([has[dy]] if dy else []) + ([hasz[dz]] if dz else []):
            ok = flag if ok is None else jnp.logical_and(ok, flag)
        return ok

    loads = [
        pltpu.make_async_copy(src.at[0], dst.at[:, pl.ds(TOP, N)], load_sem.at[i])
        for i, (src, dst) in enumerate(((classes, cl), (start, xs), (source, rh), (mults, mu)))
    ]
    small = [
        pltpu.make_async_copy(table_hbm, table, load_sem.at[4]),
        pltpu.make_async_copy(chain_hbm, chain, load_sem.at[5]),
    ]
    for copy in small + loads:
        copy.start()

    mates = {1: s + 1 - 2 * lax.rem(s, 2), 2: lax.rem(s + 2, 4), 3: 3 - s}
    mates = {pairing: mates[pairing] for pairing in (2, 1, 3) if pairing != unused}
    barrier = pltpu.get_barrier_semaphore()
    greeted = jnp.int32(len(mates))
    for dy, dz in DIRECTIONS:
        ok = there(dy, dz)
        greeted = greeted + jnp.where(ok, 1, 0)

        @pl.when(ok)
        def _(dy=dy, dz=dz):
            pl.semaphore_signal(barrier, inc=1, device_id=(s, gy + dy, gz + dz), device_id_type=MESH)

    for other in mates.values():
        pl.semaphore_signal(barrier, inc=1, device_id=(other, gy, gz), device_id_type=MESH)

    ones = jnp.ones((8, N), jnp.float32)
    zeros = jnp.zeros((8, N), jnp.float32)
    endless = jnp.full((8, N), jnp.inf, jnp.float32)
    blank = jnp.where(lanes(8) // 32 == 1, endless, zeros)
    for side, dy in ((0, -1), (1, 1)):

        @pl.when(jnp.logical_not(has[dy]))
        def _(side=side):
            for i in range(PLANES // 2):
                yrx[side, i] = endless if i in (2, 3) else zeros

        for other, dz in ((0, -1), (1, 1)):

            @pl.when(jnp.logical_not(there(dy, dz)))
            def _(k=2 * side + other):
                crx[k] = blank

    for side, dz in ((0, -1), (1, 1)):

        @pl.when(jnp.logical_not(hasz[dz]))
        def _(side=side):
            for a in range(3):
                for r in range(0, QUARTER // 2, 8):
                    zrx[side, a, pl.ds(r, 8)] = endless if a == 1 else zeros

    for r in (0, 8, BOTTOM, ROWS - 8):
        for l in range(CX):
            for ref in (xs, rh, yl, v1, v2, v3):
                ref[l, pl.ds(r, 8)] = zeros
            res[l, pl.ds(r, 8)] = endless if r in (8, BOTTOM) else ones
    for r in (0, 8 + HIGH):
        for ref in (h0, h1, h2, h3):
            ref[pl.ds(r, 8)] = zeros
        hres[pl.ds(r, 8)] = ones

    for copy in small:
        copy.wait()
    my_place = chain[s]
    lower = jnp.float32(0.0)
    upper = jnp.float32(0.0)
    for t in range(4):
        lower = lower + jnp.where(chain[t] == my_place - 1, 1.0, 0.0)
        upper = upper + jnp.where(chain[t] == my_place + 1, 1.0, 0.0)

    splats = [0.5 * inverse(jnp.full((8, N), table[i], jnp.float32)) for i in range(8)]
    splats = [v[:1] for v in splats]

    lane = lanes(QUARTER)
    group = lane // 8
    place = lane % 8

    def outer_columns(ref):
        packed = None
        for k in range(4):
            for l in range(CX):
                turned = pltpu.roll(ref[l, pl.ds(TOP + QUARTER * k, QUARTER)], QUARTER * k + 8 * l + 4, 1)
                packed = turned if packed is None else jnp.where(group == 4 * k + l, turned, packed)
        return jnp.take_along_axis(packed, lane ^ 7, axis=1)

    loads[0].wait()
    for l in range(CX):
        for r in (TOP, BOTTOM - 8):
            res[l, pl.ds(r, 8)] = lookup(cl[l, pl.ds(r, 8)], splats)
    packed_res = lookup(outer_columns(cl), splats)
    loads[1].wait()
    packed_xs = outer_columns(xs)
    loads[2].wait()
    loads[3].wait()
    rh[0, pl.ds(TOP, N)] = rh[0, pl.ds(TOP, N)] + lower * mu[0, pl.ds(TOP, N)]
    rh[CX - 1, pl.ds(TOP, N)] = rh[CX - 1, pl.ds(TOP, N)] + upper * mu[1, pl.ds(TOP, N)]
    packed_rh = outer_columns(rh)
    half = QUARTER // 2
    near_side = place[:half] < 4
    group8 = lanes(8) // 32
    up_corner = down_corner = None
    for a, packed in enumerate((packed_xs, packed_res, packed_rh)):
        ztx[0, a] = jnp.where(near_side, packed[:half], pltpu.roll(packed[half:], 4, 1))
        ztx[1, a] = jnp.where(near_side, pltpu.roll(packed[half:], N - 4, 1), packed[:half])
        first = packed[:8] if a == 0 else pltpu.roll(packed[:8], 32 * a, 1)
        final = pltpu.roll(packed[QUARTER - 8 :], 32 * a + 32, 1)
        up_corner = first if a == 0 else jnp.where(group8 == a, first, up_corner)
        down_corner = final if a == 0 else jnp.where(group8 == a, final, down_corner)
    ctx[0] = up_corner
    ctx[1] = down_corner
    planes = [(ref, l) for ref in (xs, res, rh) for l in range(CX)]
    row = lax.broadcasted_iota(jnp.int32, (8, N), 0)
    for i in range(PLANES // 2):
        (ref, l), (mate, m) = planes[2 * i], planes[2 * i + 1]
        ytx[0, i] = jnp.where(row < 4, ref[l, pl.ds(TOP, 8)], mate[m, pl.ds(TOP - 4, 8)])
        ytx[1, i] = jnp.where(row < 4, ref[l, pl.ds(BOTTOM - 4, 8)], mate[m, pl.ds(BOTTOM - 8, 8)])

    pl.semaphore_wait(barrier, greeted)

    sent = []
    for k, (dy, dz) in enumerate(DIRECTIONS):
        if dy and dz:
            src = ctx.at[0 if dy < 0 else 1]
            dst = crx.at[(2 if dy < 0 else 0) + (1 if dz < 0 else 0)]
        elif dz:
            src, dst = ztx.at[0 if dz < 0 else 1], zrx.at[1 if dz < 0 else 0]
        else:
            src, dst = ytx.at[0 if dy < 0 else 1], yrx.at[1 if dy < 0 else 0]
        copy = pltpu.make_async_remote_copy(
            src_ref=src, dst_ref=dst, send_sem=send_sem.at[k], recv_sem=recv_sem.at[k],
            device_id=(s, gy + dy, gz + dz), device_id_type=MESH,
        )
        pl.when(there(dy, dz))(copy.start)
        sent.append((copy, dy, dz))

    for l in range(CX):
        res[l, pl.ds(TOP + 8, N - 16)] = lookup(cl[l, pl.ds(TOP + 8, N - 16)], splats)

    def cat(ref, l, blocks, shift=0):
        parts = [ref[l, pl.ds(r + shift, n)] for r, n in blocks]
        return parts[0] if len(parts) == 1 else jnp.concatenate(parts, axis=0)

    def put(ref, l, blocks, value):
        at = 0
        for r, n in blocks:
            ref[l, pl.ds(r, n)] = value[at : at + n]
            at += n

    def inner_part(blocks):
        last_lane = lanes(sum(n for _, n in blocks)) == N - 1
        rc = [cat(res, l, blocks) for l in range(CX)]
        vs = [cat(xs, l, blocks) for l in range(CX)]
        links = [inverse(rc[l] + rc[l + 1]) for l in range(CX - 1)]
        for l in range(CX):
            a = inverse(rc[l] + cat(res, l, blocks, 1))
            b = inverse(rc[l] + cat(res, l, blocks, -1))
            c = jnp.where(last_lane, 0.0, inverse(rc[l] + pltpu.roll(rc[l], N - 1, 1)))
            d = pltpu.roll(c, 1, 1)
            total = CAPACITY + a + b + c + d
            near = a * cat(xs, l, blocks, 1) + b * cat(xs, l, blocks, -1)
            near = near + c * pltpu.roll(vs[l], N - 1, 1) + d * pltpu.roll(vs[l], 1, 1)
            if l > 0:
                total = total + links[l - 1]
                near = near + links[l - 1] * vs[l - 1]
            else:
                total = total + (lower * ROBIN + (1.0 - lower) * inverse(rc[l]))
            if l < CX - 1:
                total = total + links[l]
                near = near + links[l] * vs[l + 1]
                put(xl, l, blocks, links[l])
            else:
                total = total + (upper * ROBIN + (1.0 - upper) * inverse(rc[l]))
            put(yl, l, blocks, a)
            put(zn, l, blocks, c)
            put(zp, l, blocks, d)
            put(dd, l, blocks, total)
            put(rr, l, blocks, cat(rh, l, blocks) - total * vs[l] + near)

    inner_part(((TOP, N),))

    for copy, dy, dz in sent:
        pl.when(there(-dy, -dz))(copy.wait_recv)

    for side, at in ((0, TOP - 4), (1, BOTTOM)):
        for i, (ref, l) in enumerate(planes):
            ref[l, pl.ds(at, 4)] = yrx[side, i // 2, pl.ds(4 * (i % 2), 4)]

    center = (HIGH_BOUND + LOW_BOUND) / 2.0
    half_width = (HIGH_BOUND - LOW_BOUND) / 2.0
    sigma = center / half_width
    rho = 1.0 / sigma

    lane = lanes(HIGH)
    place = lane % 8
    layer = lane // 8 % 4
    near_side = lanes(half) % 8 < 4
    lane8 = lanes(8)
    near8 = lane8 % 8 < 4
    up_corner = jnp.where(near8, crx[1], crx[0])
    down_corner = jnp.where(near8, crx[3], crx[2])
    tiles = []
    for a in range(3):
        low, high = zrx[0, a], zrx[1, a]
        upper_rows = jnp.where(near_side, high, low)
        lower_rows = jnp.where(near_side, pltpu.roll(high, N - 4, 1), pltpu.roll(low, 4, 1))
        above = up_corner if a == 0 else pltpu.roll(up_corner, N - 32 * a, 1)
        above = jnp.where(lane8 < 32, above, pltpu.roll(lower_rows[half - 8 :], 32, 1))
        below = jnp.where(lane8 >= 96, pltpu.roll(down_corner, 96 - 32 * a, 1), pltpu.roll(upper_rows[:8], 96, 1))
        tiles.append(jnp.concatenate([above, upper_rows, lower_rows, below], axis=0))
    hv, hc, hrhs = tiles
    hrows = pl.ds(8, HIGH)
    hres[hrows] = hc
    h0[hrows] = hv
    gate = jnp.where((place == 3) | (place == 4), inverse(hc + edge_columns(res)), 0.0)
    hzn = jnp.where((place == 3) | (place == 7), 0.0, inverse(hc + pltpu.roll(hc, N - 1, 1)))
    hzp = pltpu.roll(hzn, 1, 1)
    hxn = jnp.where(layer < CX - 1, inverse(hc + pltpu.roll(hc, N - 8, 1)), 0.0)
    hxp = pltpu.roll(hxn, 8, 1)
    hyn = inverse(hc + hres[pl.ds(9, HIGH)])
    hyp = inverse(hc + hres[pl.ds(7, HIGH)])
    ends = inverse(hc)
    hd = CAPACITY + hyn + hyp + hzn + hzp + hxn + hxp + gate
    hd = hd + jnp.where(layer == 0, lower * ROBIN + (1.0 - lower) * ends, 0.0)
    hd = hd + jnp.where(layer == CX - 1, upper * ROBIN + (1.0 - upper) * ends, 0.0)
    he = inverse(hd)

    def outer_near(hold, hv, old):
        near = hyn * hold[pl.ds(9, HIGH)] + hyp * hold[pl.ds(7, HIGH)]
        near = near + hzn * pltpu.roll(hv, N - 1, 1) + hzp * pltpu.roll(hv, 1, 1)
        near = near + hxn * pltpu.roll(hv, N - 8, 1) + hxp * pltpu.roll(hv, 8, 1)
        return near + gate * edge_columns(old)

    hr = hrhs - hd * hv + outer_near(h0, hv, xs)
    h1[hrows] = 1.0 / center * (he * hr)

    inner_part(((FIRST, 16), (BOTTOM - 8, 16)))
    r, n = FIRST, COUNT
    lane = lanes(n)
    edge = (lane == 0) | (lane == N - 1)
    flow = gate * hv
    for l in range(CX):
        across = jnp.where(edge, turned_in(gate, l, True), 0.0)
        total = dd[l, pl.ds(r, n)] + across
        e = inverse(total)
        q = rr[l, pl.ds(r, n)] - across * xs[l, pl.ds(r, n)] + jnp.where(edge, turned_in(flow, l, True), 0.0)
        dd[l, pl.ds(r, n)] = total
        ee[l, pl.ds(r, n)] = e
        rr[l, pl.ds(r, n)] = q
        v1[l, pl.ds(r, n)] = 1.0 / center * (e * q)

    sends = []

    def send_packs(ends):
        for j, other in enumerate(mates.values()):
            above = jnp.where(chain[other] == my_place + 1, 1.0, 0.0)
            sb[j] = above * ends[1] + (1.0 - above) * ends[0]
            copy = pltpu.make_async_remote_copy(
                src_ref=sb.at[j], dst_ref=rb.at[j], send_sem=psend.at[j], recv_sem=precv.at[j],
                device_id=(other, gy, gz), device_id_type=MESH,
            )
            copy.start()
            sends.append(copy)

    steps = ((xs, h0), (v1, h1), (v2, h2), (v3, h3))
    for sweep in range(1, SWEEPS):
        rho_new = 1.0 / (2.0 * sigma - rho)
        keep, gain = rho_new * rho, 2.0 * rho_new / half_width
        rho = rho_new
        last = sweep == SWEEPS - 1
        old, hold = steps[sweep]
        if last:
            r, n = TOP, N
            lane = lanes(n)
            edge = (lane == 0) | (lane == N - 1)
        vs = [old[l, pl.ds(r, n)] for l in range(CX)]
        hv = hold[hrows]
        flow = gate * hv
        ends = []
        for l in (0, CX - 1, 1, 2):
            near = yl[l, pl.ds(r, n)] * old[l, pl.ds(r + 1, n)] + yl[l, pl.ds(r - 1, n)] * old[l, pl.ds(r - 1, n)]
            near = near + zn[l, pl.ds(r, n)] * pltpu.roll(vs[l], N - 1, 1)
            near = near + zp[l, pl.ds(r, n)] * pltpu.roll(vs[l], 1, 1)
            if l > 0:
                near = near + xl[l - 1, pl.ds(r, n)] * vs[l - 1]
            if l < CX - 1:
                near = near + xl[l, pl.ds(r, n)] * vs[l + 1]
            near = near + jnp.where(edge, turned_in(flow, l, not last), 0.0)
            q = rr[l, pl.ds(r, n)] - dd[l, pl.ds(r, n)] * vs[l] + near
            step = keep * vs[l] + gain * (ee[l, pl.ds(r, n)] * q)
            if last:
                field = xs[l, pl.ds(r, n)] + v1[l, pl.ds(r, n)] + v2[l, pl.ds(r, n)]
                field = field + (vs[l] + step)
                t_out[0, l] = field
                if l == 0:
                    ends.append(2.0 * ROBIN * field - mu[0, pl.ds(r, n)])
                if l == CX - 1:
                    ends.append(2.0 * ROBIN * field - mu[1, pl.ds(r, n)])
                    send_packs(ends)
            else:
                rr[l, pl.ds(r, n)] = q
                steps[sweep + 1][0][l, pl.ds(r, n)] = step
        if not last:
            hr = hr - hd * hv + outer_near(hold, hv, old)
            steps[sweep + 1][1][hrows] = keep * hv + gain * (he * hr)

    for copy, dy, dz in sent:
        pl.when(there(dy, dz))(copy.wait_send)
    for copy in sends:
        copy.wait_recv()
    for side, shift in ((0, -1), (1, 1)):
        total = None
        for j, other in enumerate(mates.values()):
            mine = jnp.where(chain[other] == my_place + shift, 1.0, 0.0) * rb[j]
            total = mine if total is None else total + mine
        m_out[0, side] = total
    for copy in sends:
        copy.wait_send()


def call(unused, arrays):
    wide = pltpu.VMEM((CX, ROWS, N), jnp.float32)
    tall = pltpu.VMEM((HIGH + 16, N), jnp.float32)
    outside = pl.BlockSpec(memory_space=pltpu.HBM)
    inside = pl.BlockSpec(memory_space=pltpu.VMEM)
    arrays = [pltpu.with_memory_space_constraint(x, pltpu.HBM) for x in arrays]
    return pl.pallas_call(
        functools.partial(kernel, unused),
        out_shape=(
            pltpu.VMEM((1, CX, N, N), jnp.float32),
            pltpu.VMEM((1, 2, N, N), jnp.float32),
        ),
        in_specs=[outside] * 6,
        out_specs=(inside, inside),
        scratch_shapes=[
            pltpu.SMEM((8,), jnp.float32), pltpu.SMEM((4,), jnp.int32),
            wide, pltpu.VMEM((CX, ROWS, N), jnp.int32), wide, pltpu.VMEM((2, ROWS, N), jnp.float32), wide,
            pltpu.VMEM((2, 8, N), jnp.float32), pltpu.VMEM((4, 8, N), jnp.float32),
            pltpu.VMEM((2, 3, QUARTER // 2, N), jnp.float32), pltpu.VMEM((2, 3, QUARTER // 2, N), jnp.float32),
            pltpu.VMEM((2, PLANES // 2, 8, N), jnp.float32), pltpu.VMEM((2, PLANES // 2, 8, N), jnp.float32),
            wide, wide, wide, wide, wide, wide, wide, wide, wide, wide, tall, tall, tall, tall, tall,
            pltpu.VMEM((2, N, N), jnp.float32), pltpu.VMEM((2, N, N), jnp.float32),
            pltpu.SemaphoreType.DMA((6,)), pltpu.SemaphoreType.DMA((8,)), pltpu.SemaphoreType.DMA((8,)),
            pltpu.SemaphoreType.DMA((2,)), pltpu.SemaphoreType.DMA((2,)),
        ],
        compiler_params=pltpu.CompilerParams(
            collective_id=unused - 1, has_side_effects=True, vmem_limit_bytes=32 * 1024 * 1024
        ),
    )(*arrays)


def pick(chain_hbm, out, chain, sem):
    copy = pltpu.make_async_copy(chain_hbm, chain, sem)
    copy.start()
    copy.wait()
    out[0] = jnp.int32(0)
    for t in range(2, 4):

        @pl.when(jnp.abs(chain[t] - chain[0]) == 2)
        def _(t=t):
            out[0] = jnp.int32(t - 1)


def shards(source, start_field, classes, class_table, chain_place, multipliers):
    arrays = (source, start_field, classes, class_table, chain_place, multipliers)
    chain_place = pltpu.with_memory_space_constraint(chain_place, pltpu.HBM)
    unused = pl.pallas_call(
        pick,
        out_shape=pltpu.SMEM((1,), jnp.int32),
        in_specs=[pl.BlockSpec(memory_space=pltpu.HBM)],
        out_specs=pl.BlockSpec(memory_space=pltpu.SMEM),
        scratch_shapes=[pltpu.SMEM((4,), jnp.int32), pltpu.SemaphoreType.DMA],
    )(chain_place)
    branches = [functools.partial(call, pairing) for pairing in (1, 2, 3)]
    return lax.switch(unused[0], branches, arrays)


def solution(mesh):
    blocks = P("sub", None, "gy", "gz")
    return jax.shard_map(
        shards,
        mesh=mesh,
        in_specs=(blocks, blocks, blocks, P(), P(), blocks),
        out_specs=(blocks, blocks),
        check_vma=False,
    )
```

```python
import functools

import jax
import jax.numpy as jnp
from jax import lax
from jax.experimental import pallas as pl
from jax.experimental.pallas import tpu as pltpu
from jax.sharding import PartitionSpec as P

SWEEPS = 4
ROBIN = 1.0
CAPACITY = 0.5
LOW_BOUND = 0.1
HIGH_BOUND = 2.0
MESH = pl.DeviceIdType.MESH

CX = 4
N = 128
TOP = 16
BOTTOM = TOP + N
ROWS = BOTTOM + 16
FIRST, COUNT = 8, N + 16
QUARTER = N // 4
HIGH = QUARTER + 16
JOINED = ((1, 3, None), (2, 1, None), (2, 3, None), (1, 2, False), (1, 2, True), (3, 2, False), (3, 2, True))
PLANES = 12
DIRECTIONS = ((-1, -1), (-1, 1), (1, -1), (1, 1), (0, 1), (0, -1), (-1, 0), (1, 0))


def inverse(x):
    return pltpu.reciprocal(x, approx=True)


def lookup(classes, splats):
    bit0 = (classes & 1) == 1
    bit1 = (classes & 2) == 2
    bit2 = classes >= 4
    pairs = [jnp.where(bit0, splats[i + 1], splats[i]) for i in range(0, 8, 2)]
    quads = [jnp.where(bit1, pairs[i + 1], pairs[i]) for i in (0, 2)]
    return jnp.where(bit2, quads[1], quads[0])


def lanes(n):
    return lax.broadcasted_iota(jnp.int32, (n, N), 1)


def edge_columns(ref):
    group = lanes(QUARTER) // 8
    body = None
    for k in range(4):
        for l in range(CX):
            turned = pltpu.roll(ref[l, pl.ds(TOP + QUARTER * k, QUARTER)], QUARTER * k + 8 * l + 4, 1)
            body = turned if body is None else jnp.where(group == 4 * k + l, turned, body)
    group = lanes(8) // 8
    above = pltpu.roll(body[QUARTER - 8 :], QUARTER, 1)
    below = pltpu.roll(body[:8], N - QUARTER, 1)
    for l in range(CX):
        above = jnp.where(group == l, pltpu.roll(ref[l, pl.ds(TOP - 8, 8)], 8 * l + 4, 1), above)
        below = jnp.where(group == 12 + l, pltpu.roll(ref[l, pl.ds(BOTTOM, 8)], 96 + 8 * l + 4, 1), below)
    return jnp.concatenate([above, body, below], axis=0)


def turned_in(h, l, whole):
    parts = [pltpu.roll(h[8 : 8 + QUARTER], N - (QUARTER * k + 8 * l + 4), 1) for k in range(4)]
    if whole:
        above = pltpu.roll(h[:8], N - (8 * l + 4), 1)
        below = pltpu.roll(h[8 + QUARTER :], N - (96 + 8 * l + 4), 1)
        parts = [above] + parts + [below]
    return jnp.concatenate(parts, axis=0)


def kernel(
    joined, source, start, classes, table_hbm, chain_hbm, mults, t_out, m_out,
    table, chain, xs, cl, rh, mu, res, ctx, crx, ztx, zrx, ytx, yrx,
    yl, zn, zp, xl, dd, ee, rr, v1, v2, v3, hres, h0, h1, h2, h3, sb, rb,
    load_sem, send_sem, recv_sem, psend, precv,
):
    s = lax.axis_index("sub")
    gy = lax.axis_index("gy")
    gz = lax.axis_index("gz")
    ny = lax.axis_size("gy")
    nz = lax.axis_size("gz")
    has = {-1: gy > 0, 1: gy < ny - 1}
    hasz = {-1: gz > 0, 1: gz < nz - 1}

    def there(dy, dz):
        ok = None
        for flag in ([has[dy]] if dy else []) + ([hasz[dz]] if dz else []):
            ok = flag if ok is None else jnp.logical_and(ok, flag)
        return ok

    loads = [
        pltpu.make_async_copy(src.at[0], dst.at[:, pl.ds(TOP, N)], load_sem.at[i])
        for i, (src, dst) in enumerate(((classes, cl), (start, xs), (source, rh), (mults, mu)))
    ]
    small = [
        pltpu.make_async_copy(table_hbm, table, load_sem.at[4]),
        pltpu.make_async_copy(chain_hbm, chain, load_sem.at[5]),
    ]
    for copy in small + loads:
        copy.start()

    both, single, with_first = joined
    mates = {1: s + 1 - 2 * lax.rem(s, 2), 2: lax.rem(s + 2, 4), 3: 3 - s}
    in_first = jnp.logical_or(s == 0, s == single)
    paired = None if with_first is None else in_first if with_first else jnp.logical_not(in_first)
    mates = [(way, mates[way], paired if way == single else None) for way in (2, 1, 3) if way in (both, single)]

    def where_paired(ok, action):
        if ok is None:
            action()
        else:
            pl.when(ok)(action)

    barrier = pltpu.get_barrier_semaphore()
    greeted = jnp.int32(2) if paired is None else jnp.where(paired, 2, 1)
    for dy, dz in DIRECTIONS:
        ok = there(dy, dz)
        greeted = greeted + jnp.where(ok, 1, 0)

        @pl.when(ok)
        def _(dy=dy, dz=dz):
            pl.semaphore_signal(barrier, inc=1, device_id=(s, gy + dy, gz + dz), device_id_type=MESH)

    for j, (way, other, ok) in enumerate(mates):

        def greet(other=other):
            pl.semaphore_signal(barrier, inc=1, device_id=(other, gy, gz), device_id_type=MESH)

        where_paired(ok, greet)
        if ok is not None:

            @pl.when(jnp.logical_not(ok))
            def _(j=j):
                for r in range(0, N, 8):
                    rb[j, pl.ds(r, 8)] = jnp.zeros((8, N), jnp.float32)


    ones = jnp.ones((8, N), jnp.float32)
    zeros = jnp.zeros((8, N), jnp.float32)
    endless = jnp.full((8, N), jnp.inf, jnp.float32)
    blank = jnp.where(lanes(8) // 32 == 1, endless, zeros)
    for side, dy in ((0, -1), (1, 1)):

        @pl.when(jnp.logical_not(has[dy]))
        def _(side=side):
            for i in range(PLANES // 2):
                yrx[side, i] = endless if i in (2, 3) else zeros

        for other, dz in ((0, -1), (1, 1)):

            @pl.when(jnp.logical_not(there(dy, dz)))
            def _(k=2 * side + other):
                crx[k] = blank

    for side, dz in ((0, -1), (1, 1)):

        @pl.when(jnp.logical_not(hasz[dz]))
        def _(side=side):
            for a in range(3):
                for r in range(0, QUARTER // 2, 8):
                    zrx[side, a, pl.ds(r, 8)] = endless if a == 1 else zeros

    for r in (0, 8, BOTTOM, ROWS - 8):
        for l in range(CX):
            for ref in (xs, rh, yl, v1, v2, v3):
                ref[l, pl.ds(r, 8)] = zeros
            res[l, pl.ds(r, 8)] = endless if r in (8, BOTTOM) else ones
    for r in (0, 8 + HIGH):
        for ref in (h0, h1, h2, h3):
            ref[pl.ds(r, 8)] = zeros
        hres[pl.ds(r, 8)] = ones

    for copy in small:
        copy.wait()
    my_place = chain[s]
    lower = jnp.float32(0.0)
    upper = jnp.float32(0.0)
    for t in range(4):
        lower = lower + jnp.where(chain[t] == my_place - 1, 1.0, 0.0)
        upper = upper + jnp.where(chain[t] == my_place + 1, 1.0, 0.0)

    splats = [0.5 * inverse(jnp.full((8, N), table[i], jnp.float32)) for i in range(8)]
    splats = [v[:1] for v in splats]

    lane = lanes(QUARTER)
    group = lane // 8
    place = lane % 8

    def outer_columns(ref):
        packed = None
        for k in range(4):
            for l in range(CX):
                turned = pltpu.roll(ref[l, pl.ds(TOP + QUARTER * k, QUARTER)], QUARTER * k + 8 * l + 4, 1)
                packed = turned if packed is None else jnp.where(group == 4 * k + l, turned, packed)
        return jnp.take_along_axis(packed, lane ^ 7, axis=1)

    loads[0].wait()
    for l in range(CX):
        for r in (TOP, BOTTOM - 8):
            res[l, pl.ds(r, 8)] = lookup(cl[l, pl.ds(r, 8)], splats)
    packed_res = lookup(outer_columns(cl), splats)
    loads[1].wait()
    packed_xs = outer_columns(xs)
    loads[2].wait()
    loads[3].wait()
    rh[0, pl.ds(TOP, N)] = rh[0, pl.ds(TOP, N)] + lower * mu[0, pl.ds(TOP, N)]
    rh[CX - 1, pl.ds(TOP, N)] = rh[CX - 1, pl.ds(TOP, N)] + upper * mu[1, pl.ds(TOP, N)]
    packed_rh = outer_columns(rh)
    half = QUARTER // 2
    near_side = place[:half] < 4
    group8 = lanes(8) // 32
    up_corner = down_corner = None
    for a, packed in enumerate((packed_xs, packed_res, packed_rh)):
        ztx[0, a] = jnp.where(near_side, packed[:half], pltpu.roll(packed[half:], 4, 1))
        ztx[1, a] = jnp.where(near_side, pltpu.roll(packed[half:], N - 4, 1), packed[:half])
        first = packed[:8] if a == 0 else pltpu.roll(packed[:8], 32 * a, 1)
        final = pltpu.roll(packed[QUARTER - 8 :], 32 * a + 32, 1)
        up_corner = first if a == 0 else jnp.where(group8 == a, first, up_corner)
        down_corner = final if a == 0 else jnp.where(group8 == a, final, down_corner)
    ctx[0] = up_corner
    ctx[1] = down_corner
    planes = [(ref, l) for ref in (xs, res, rh) for l in range(CX)]
    row = lax.broadcasted_iota(jnp.int32, (8, N), 0)
    for i in range(PLANES // 2):
        (ref, l), (mate, m) = planes[2 * i], planes[2 * i + 1]
        ytx[0, i] = jnp.where(row < 4, ref[l, pl.ds(TOP, 8)], mate[m, pl.ds(TOP - 4, 8)])
        ytx[1, i] = jnp.where(row < 4, ref[l, pl.ds(BOTTOM - 4, 8)], mate[m, pl.ds(BOTTOM - 8, 8)])

    pl.semaphore_wait(barrier, greeted)

    sent = []
    for k, (dy, dz) in enumerate(DIRECTIONS):
        if dy and dz:
            src = ctx.at[0 if dy < 0 else 1]
            dst = crx.at[(2 if dy < 0 else 0) + (1 if dz < 0 else 0)]
        elif dz:
            src, dst = ztx.at[0 if dz < 0 else 1], zrx.at[1 if dz < 0 else 0]
        else:
            src, dst = ytx.at[0 if dy < 0 else 1], yrx.at[1 if dy < 0 else 0]
        copy = pltpu.make_async_remote_copy(
            src_ref=src, dst_ref=dst, send_sem=send_sem.at[k], recv_sem=recv_sem.at[k],
            device_id=(s, gy + dy, gz + dz), device_id_type=MESH,
        )
        pl.when(there(dy, dz))(copy.start)
        sent.append((copy, dy, dz))

    for l in range(CX):
        res[l, pl.ds(TOP + 8, N - 16)] = lookup(cl[l, pl.ds(TOP + 8, N - 16)], splats)

    def cat(ref, l, blocks, shift=0):
        parts = [ref[l, pl.ds(r + shift, n)] for r, n in blocks]
        return parts[0] if len(parts) == 1 else jnp.concatenate(parts, axis=0)

    def put(ref, l, blocks, value):
        at = 0
        for r, n in blocks:
            ref[l, pl.ds(r, n)] = value[at : at + n]
            at += n

    def inner_part(blocks):
        last_lane = lanes(sum(n for _, n in blocks)) == N - 1
        rc = [cat(res, l, blocks) for l in range(CX)]
        vs = [cat(xs, l, blocks) for l in range(CX)]
        links = [inverse(rc[l] + rc[l + 1]) for l in range(CX - 1)]
        for l in range(CX):
            a = inverse(rc[l] + cat(res, l, blocks, 1))
            b = inverse(rc[l] + cat(res, l, blocks, -1))
            c = jnp.where(last_lane, 0.0, inverse(rc[l] + pltpu.roll(rc[l], N - 1, 1)))
            d = pltpu.roll(c, 1, 1)
            total = CAPACITY + a + b + c + d
            near = a * cat(xs, l, blocks, 1) + b * cat(xs, l, blocks, -1)
            near = near + c * pltpu.roll(vs[l], N - 1, 1) + d * pltpu.roll(vs[l], 1, 1)
            if l > 0:
                total = total + links[l - 1]
                near = near + links[l - 1] * vs[l - 1]
            else:
                total = total + (lower * ROBIN + (1.0 - lower) * inverse(rc[l]))
            if l < CX - 1:
                total = total + links[l]
                near = near + links[l] * vs[l + 1]
                put(xl, l, blocks, links[l])
            else:
                total = total + (upper * ROBIN + (1.0 - upper) * inverse(rc[l]))
            put(yl, l, blocks, a)
            put(zn, l, blocks, c)
            put(zp, l, blocks, d)
            put(dd, l, blocks, total)
            put(rr, l, blocks, cat(rh, l, blocks) - total * vs[l] + near)

    inner_part(((TOP, N),))

    for copy, dy, dz in sent:
        pl.when(there(-dy, -dz))(copy.wait_recv)

    for side, at in ((0, TOP - 4), (1, BOTTOM)):
        for i, (ref, l) in enumerate(planes):
            ref[l, pl.ds(at, 4)] = yrx[side, i // 2, pl.ds(4 * (i % 2), 4)]

    center = (HIGH_BOUND + LOW_BOUND) / 2.0
    half_width = (HIGH_BOUND - LOW_BOUND) / 2.0
    sigma = center / half_width
    rho = 1.0 / sigma

    lane = lanes(HIGH)
    place = lane % 8
    layer = lane // 8 % 4
    near_side = lanes(half) % 8 < 4
    lane8 = lanes(8)
    near8 = lane8 % 8 < 4
    up_corner = jnp.where(near8, crx[1], crx[0])
    down_corner = jnp.where(near8, crx[3], crx[2])
    tiles = []
    for a in range(3):
        low, high = zrx[0, a], zrx[1, a]
        upper_rows = jnp.where(near_side, high, low)
        lower_rows = jnp.where(near_side, pltpu.roll(high, N - 4, 1), pltpu.roll(low, 4, 1))
        above = up_corner if a == 0 else pltpu.roll(up_corner, N - 32 * a, 1)
        above = jnp.where(lane8 < 32, above, pltpu.roll(lower_rows[half - 8 :], 32, 1))
        below = jnp.where(lane8 >= 96, pltpu.roll(down_corner, 96 - 32 * a, 1), pltpu.roll(upper_rows[:8], 96, 1))
        tiles.append(jnp.concatenate([above, upper_rows, lower_rows, below], axis=0))
    hv, hc, hrhs = tiles
    hrows = pl.ds(8, HIGH)
    hres[hrows] = hc
    h0[hrows] = hv
    gate = jnp.where((place == 3) | (place == 4), inverse(hc + edge_columns(res)), 0.0)
    hzn = jnp.where((place == 3) | (place == 7), 0.0, inverse(hc + pltpu.roll(hc, N - 1, 1)))
    hzp = pltpu.roll(hzn, 1, 1)
    hxn = jnp.where(layer < CX - 1, inverse(hc + pltpu.roll(hc, N - 8, 1)), 0.0)
    hxp = pltpu.roll(hxn, 8, 1)
    hyn = inverse(hc + hres[pl.ds(9, HIGH)])
    hyp = inverse(hc + hres[pl.ds(7, HIGH)])
    ends = inverse(hc)
    hd = CAPACITY + hyn + hyp + hzn + hzp + hxn + hxp + gate
    hd = hd + jnp.where(layer == 0, lower * ROBIN + (1.0 - lower) * ends, 0.0)
    hd = hd + jnp.where(layer == CX - 1, upper * ROBIN + (1.0 - upper) * ends, 0.0)
    he = inverse(hd)

    def outer_near(hold, hv, old):
        near = hyn * hold[pl.ds(9, HIGH)] + hyp * hold[pl.ds(7, HIGH)]
        near = near + hzn * pltpu.roll(hv, N - 1, 1) + hzp * pltpu.roll(hv, 1, 1)
        near = near + hxn * pltpu.roll(hv, N - 8, 1) + hxp * pltpu.roll(hv, 8, 1)
        return near + gate * edge_columns(old)

    hr = hrhs - hd * hv + outer_near(h0, hv, xs)
    h1[hrows] = 1.0 / center * (he * hr)

    inner_part(((FIRST, 16), (BOTTOM - 8, 16)))
    r, n = FIRST, COUNT
    lane = lanes(n)
    edge = (lane == 0) | (lane == N - 1)
    flow = gate * hv
    for l in range(CX):
        across = jnp.where(edge, turned_in(gate, l, True), 0.0)
        total = dd[l, pl.ds(r, n)] + across
        e = inverse(total)
        q = rr[l, pl.ds(r, n)] - across * xs[l, pl.ds(r, n)] + jnp.where(edge, turned_in(flow, l, True), 0.0)
        dd[l, pl.ds(r, n)] = total
        ee[l, pl.ds(r, n)] = e
        rr[l, pl.ds(r, n)] = q
        v1[l, pl.ds(r, n)] = 1.0 / center * (e * q)

    sends = []

    def send_packs(ends):
        for j, (way, other, ok) in enumerate(mates):
            above = jnp.where(chain[other] == my_place + 1, 1.0, 0.0)
            sb[j] = above * ends[1] + (1.0 - above) * ends[0]
            copy = pltpu.make_async_remote_copy(
                src_ref=sb.at[j], dst_ref=rb.at[j], send_sem=psend.at[j], recv_sem=precv.at[j],
                device_id=(other, gy, gz), device_id_type=MESH,
            )
            where_paired(ok, copy.start)
            sends.append((copy, ok))

    steps = ((xs, h0), (v1, h1), (v2, h2), (v3, h3))
    for sweep in range(1, SWEEPS):
        rho_new = 1.0 / (2.0 * sigma - rho)
        keep, gain = rho_new * rho, 2.0 * rho_new / half_width
        rho = rho_new
        last = sweep == SWEEPS - 1
        old, hold = steps[sweep]
        if last:
            r, n = TOP, N
            lane = lanes(n)
            edge = (lane == 0) | (lane == N - 1)
        vs = [old[l, pl.ds(r, n)] for l in range(CX)]
        hv = hold[hrows]
        flow = gate * hv
        ends = []
        for l in (0, CX - 1, 1, 2):
            near = yl[l, pl.ds(r, n)] * old[l, pl.ds(r + 1, n)] + yl[l, pl.ds(r - 1, n)] * old[l, pl.ds(r - 1, n)]
            near = near + zn[l, pl.ds(r, n)] * pltpu.roll(vs[l], N - 1, 1)
            near = near + zp[l, pl.ds(r, n)] * pltpu.roll(vs[l], 1, 1)
            if l > 0:
                near = near + xl[l - 1, pl.ds(r, n)] * vs[l - 1]
            if l < CX - 1:
                near = near + xl[l, pl.ds(r, n)] * vs[l + 1]
            near = near + jnp.where(edge, turned_in(flow, l, not last), 0.0)
            q = rr[l, pl.ds(r, n)] - dd[l, pl.ds(r, n)] * vs[l] + near
            step = keep * vs[l] + gain * (ee[l, pl.ds(r, n)] * q)
            if last:
                field = xs[l, pl.ds(r, n)] + v1[l, pl.ds(r, n)] + v2[l, pl.ds(r, n)]
                field = field + (vs[l] + step)
                t_out[0, l] = field
                if l == 0:
                    ends.append(2.0 * ROBIN * field - mu[0, pl.ds(r, n)])
                if l == CX - 1:
                    ends.append(2.0 * ROBIN * field - mu[1, pl.ds(r, n)])
                    send_packs(ends)
            else:
                rr[l, pl.ds(r, n)] = q
                steps[sweep + 1][0][l, pl.ds(r, n)] = step
        if not last:
            hr = hr - hd * hv + outer_near(hold, hv, old)
            steps[sweep + 1][1][hrows] = keep * hv + gain * (he * hr)

    for copy, dy, dz in sent:
        pl.when(there(dy, dz))(copy.wait_send)
    for copy, ok in sends:
        where_paired(ok, copy.wait_recv)
    for side, shift in ((0, -1), (1, 1)):
        total = None
        for j, (way, other, ok) in enumerate(mates):
            mine = jnp.where(chain[other] == my_place + shift, 1.0, 0.0) * rb[j]
            total = mine if total is None else total + mine
        m_out[0, side] = total
    for copy, ok in sends:
        where_paired(ok, copy.wait_send)


def call(index, joined, arrays):
    wide = pltpu.VMEM((CX, ROWS, N), jnp.float32)
    tall = pltpu.VMEM((HIGH + 16, N), jnp.float32)
    outside = pl.BlockSpec(memory_space=pltpu.HBM)
    inside = pl.BlockSpec(memory_space=pltpu.VMEM)
    arrays = [pltpu.with_memory_space_constraint(x, pltpu.HBM) for x in arrays]
    return pl.pallas_call(
        functools.partial(kernel, joined),
        out_shape=(
            pltpu.VMEM((1, CX, N, N), jnp.float32),
            pltpu.VMEM((1, 2, N, N), jnp.float32),
        ),
        in_specs=[outside] * 6,
        out_specs=(inside, inside),
        scratch_shapes=[
            pltpu.SMEM((8,), jnp.float32), pltpu.SMEM((4,), jnp.int32),
            wide, pltpu.VMEM((CX, ROWS, N), jnp.int32), wide, pltpu.VMEM((2, ROWS, N), jnp.float32), wide,
            pltpu.VMEM((2, 8, N), jnp.float32), pltpu.VMEM((4, 8, N), jnp.float32),
            pltpu.VMEM((2, 3, QUARTER // 2, N), jnp.float32), pltpu.VMEM((2, 3, QUARTER // 2, N), jnp.float32),
            pltpu.VMEM((2, PLANES // 2, 8, N), jnp.float32), pltpu.VMEM((2, PLANES // 2, 8, N), jnp.float32),
            wide, wide, wide, wide, wide, wide, wide, wide, wide, wide, tall, tall, tall, tall, tall,
            pltpu.VMEM((2, N, N), jnp.float32), pltpu.VMEM((2, N, N), jnp.float32),
            pltpu.SemaphoreType.DMA((6,)), pltpu.SemaphoreType.DMA((8,)), pltpu.SemaphoreType.DMA((8,)),
            pltpu.SemaphoreType.DMA((2,)), pltpu.SemaphoreType.DMA((2,)),
        ],
        compiler_params=pltpu.CompilerParams(
            collective_id=index, has_side_effects=True, vmem_limit_bytes=32 * 1024 * 1024
        ),
    )(*arrays)


def pick(chain_hbm, out, chain, sem):
    copy = pltpu.make_async_copy(chain_hbm, chain, sem)
    copy.start()
    copy.wait()
    first = chain[0]
    both = single = jnp.int32(0)
    for t in range(1, 4):
        both = both + jnp.where(chain[t] == first + 1 - 2 * (first % 2), t, 0)
        single = single + jnp.where(chain[t] == 3 - first, t, 0)
    with_first = jnp.where((first == 1) | (first == 2), 1, 0)
    crossing = 2 + both + with_first
    out[0] = jnp.where(single == 2, crossing, jnp.where(both == 2, (single + 1) // 2, 0))


def shards(source, start_field, classes, class_table, chain_place, multipliers):
    arrays = (source, start_field, classes, class_table, chain_place, multipliers)
    choice = pl.pallas_call(
        pick,
        out_shape=pltpu.SMEM((1,), jnp.int32),
        in_specs=[pl.BlockSpec(memory_space=pltpu.HBM)],
        out_specs=pl.BlockSpec(memory_space=pltpu.SMEM),
        scratch_shapes=[pltpu.SMEM((4,), jnp.int32), pltpu.SemaphoreType.DMA],
    )(chain_place)
    branches = [functools.partial(call, index, joined) for index, joined in enumerate(JOINED)]
    return lax.switch(choice[0], branches, arrays)


def solution(mesh):
    blocks = P("sub", None, "gy", "gz")
    return jax.shard_map(
        shards,
        mesh=mesh,
        in_specs=(blocks, blocks, blocks, P(), P(), blocks),
        out_specs=(blocks, blocks),
        check_vma=False,
    )
```
